512 devices in a mesh: tm: 16 (over y, core), rows: 32 (over z, x).
Axes of the slice: x: 4, y: 8, z: 8, core: 2. Of those that a mesh axis runs over, the one named last changes fastest.
Arguments:
- latent: bfloat16 [32, 128, 16, 384], P('tm', 'rows'), may hold values from -6 to 6
- gain_first: float32 [384], replicated, may hold values from 0.5 to 2
- conv_first: bfloat16 [27, 384, 384], P(None, 'tm'), may hold values from -0.0625 to 0.0625
- bias_first: float32 [384], replicated, may hold values from -0.5 to 0.5
- conv_upper: bfloat16 [9, 384, 192], replicated, may hold values from -0.109375 to 0.109375
- bias_upper: float32 [192], replicated, may hold values from -0.5 to 0.5
Outputs:
- decoded: bfloat16 [32, 256, 6144], P('tm', 'rows')
The draws below stay inside these ranges and needn't reach their ends.
All inputs are finite; a program needn't handle non-finite values.
Results may differ from the reference program's by a relative error of at most 0.0052.
Values may be sent and summed in bfloat16 or wider, within the bound.
No kernel may reach another device: no remote copies, remote signals or barrier semaphores. Data moves between devices by JAX's collectives and lax.ppermute only.
A program may use at most 64 MiB of HBM per device.

```python
import math
import jax
import jax.numpy as jnp
from jax import lax

C = 384
CO = 192
W = 16
NT = 32
NH = 128


def level_of(key, shape, split, smallest, high):
    def one(axis_at, parts):
        draws = jax.random.uniform(jax.random.fold_in(jax.random.fold_in(key, 6), axis_at), (parts,), jnp.float32, smallest / len(split), high / len(split))
        return jnp.repeat(jnp.exp(draws), shape[axis_at] // parts).reshape((-1,) + (1,) * (len(shape) - axis_at - 1))

    level = one(*split[0])
    for cut in split[1:]:
        level = level * one(*cut)
    return level


def scatter_about(key, dims, scale, most, split=(), kind=jnp.bfloat16):
    loudness = level_of(key, dims, split, -0.22, 0.18) if split else 1.0
    values = jax.random.normal(key, dims, jnp.float32) * scale * loudness
    return jnp.minimum(jnp.maximum(values, -most), most).astype(kind)


def setup_inputs(seed: int = 0) -> dict:
    key_list = jax.random.split(jax.random.key(seed), 7)
    latent = scatter_about(key_list[0], (NT, NH, W, C), 1.0, 6.0, ((0, 16), (1, 32)))
    gain_first = jnp.clip(jnp.exp(jax.random.uniform(key_list[1], (C,), jnp.float32, math.log(0.5), math.log(2.0))), 0.5, 2.0)
    conv_first = scatter_about(key_list[2], (27, C, C), (27 * C) ** -0.5, 0.0625, ((1, 16),))
    bias_first = jnp.clip(jax.random.uniform(key_list[3], (C,), jnp.float32, -0.5, 0.5), -0.5, 0.5)
    conv_upper = scatter_about(key_list[4], (9, C, CO), (9 * C) ** -0.5, 0.109375)
    bias_upper = jnp.clip(jax.random.uniform(key_list[5], (CO,), jnp.float32, -0.5, 0.5), -0.5, 0.5)
    return {"latent": latent, "gain_first": gain_first, "conv_first": conv_first, "bias_first": bias_first, "conv_upper": conv_upper, "bias_upper": bias_upper}


def scaled_silu(features, gain):
    values = features.astype(jnp.float32)
    mean_square = lax.optimization_barrier(jnp.mean(values * values, axis=-1, keepdims=True))
    scaled = values * lax.rsqrt(mean_square + 1e-06) * gain.astype(jnp.float32)
    return (scaled * jax.nn.sigmoid(scaled)).astype(jnp.bfloat16)

def causal_conv(activated, kernel, bias):
    chans = activated.shape[-1]
    values = activated.astype(jnp.float32)
    padded = jnp.pad(values, ((2, 0), (1, 1), (1, 1), (0, 0)))
    weights = kernel.astype(jnp.float32).reshape(3, 3, 3, chans, kernel.shape[-1])
    result = lax.conv_general_dilated(padded[None], weights, (1, 1, 1), 'VALID', dimension_numbers=('NDHWC', 'DHWIO', 'NDHWC'), precision=lax.Precision.HIGHEST)[0]
    return result + bias.astype(jnp.float32)

def reference(latent, gain_first, conv_first, bias_first, conv_upper, bias_upper):
    first_act = scaled_silu(latent, gain_first)
    conv_out = causal_conv(first_act, conv_first, bias_first)
    block_out = (latent.astype(jnp.float32) + conv_out).astype(jnp.bfloat16)
    chans = conv_upper.shape[1]
    outputs = conv_upper.shape[2]
    upper_weights = conv_upper.astype(jnp.float32).reshape(3, 3, chans, outputs)

    def one_frame(frame):
        values = frame.astype(jnp.float32)
        larger = jnp.repeat(jnp.repeat(values, 2, axis=0), 2, axis=1)
        result = lax.conv_general_dilated(larger[None], upper_weights, (1, 1), ((1, 1), (1, 1)), dimension_numbers=('NHWC', 'HWIO', 'NHWC'), precision=lax.Precision.HIGHEST)[0]
        result = (result + bias_upper.astype(jnp.float32)).astype(jnp.bfloat16)
        return result.reshape(result.shape[0], result.shape[1] * result.shape[2])
    return lax.map(one_frame, block_out)
```

```python
import jax
import jax.numpy as jnp
import numpy as np
from jax import lax
from jax.experimental import pallas as pl
from jax.experimental.pallas import tpu as pltpu
from jax.sharding import Mesh
from jax.sharding import PartitionSpec as P

F32 = jnp.float32
BF16 = jnp.bfloat16
FRAMES, ROWS, COLS, CHANS, OUTS = 2, 4, 16, 384, 192
LINE = 8
PART = CHANS // LINE
CELLS = FRAMES * ROWS * COLS
BORDERED = FRAMES * (ROWS + 2) * COLS
NT_DIMS = (((1,), (1,)), ((), ()))
TN_DIMS = (((0,), (0,)), ((), ()))
PARAMS = pltpu.CompilerParams(vmem_limit_bytes=40 * 1024 * 1024)


def window_picks():
    picks = np.zeros((3, BORDERED, 9, FRAMES, ROWS, COLS), np.float32)
    for dy in range(3):
        for dx in range(3):
            for r in range(ROWS):
                for c in range(COLS):
                    col = c + dx - 1
                    if 0 <= col < COLS:
                        for f in range(FRAMES):
                            cell = f * (ROWS + 2) * COLS + (r + dy) * COLS + col
                            picks[0, cell, 3 * dy + dx, f, r, c] = 1
                            picks[1 if f == 0 else 2, cell, 3 * dy + dx, 1 - f, r, c] = 1
    return picks.reshape(3, BORDERED, 9 * CELLS)


def row_picks():
    picks = np.zeros((3, COLS, FRAMES, 2 * ROWS, FRAMES, ROWS + 2, COLS), np.float32)
    for dy in range(3):
        for i in range(2 * ROWS):
            row = (i + dy - 1) // 2 + 1
            for f in range(FRAMES):
                for c in range(COLS):
                    picks[dy, c, f, i, f, row, c] = 1
    return picks.reshape(3 * COLS * FRAMES * 2 * ROWS, BORDERED)


def act_kernel(up_ref, lat_ref, down_ref, gain_ref, out_ref):
    pieces = []
    for f in range(FRAMES):
        pieces += [up_ref[f], lat_ref[f].reshape(ROWS * COLS, CHANS), down_ref[f]]
    values = jnp.concatenate(pieces, axis=0).astype(F32)
    mean_square = jnp.mean(values * values, axis=-1, keepdims=True)
    scaled = values * lax.rsqrt(mean_square + 1e-06) * gain_ref[...]
    act = (scaled / (1.0 + jnp.exp(-scaled))).astype(BF16)
    row = lax.broadcasted_iota(jnp.int32, (CHANS, CHANS), 0)
    col = lax.broadcasted_iota(jnp.int32, (CHANS, CHANS), 1)
    eye = jnp.where(row == col, 1.0, 0.0).astype(BF16)
    flipped = lax.dot_general(eye, act, NT_DIMS, preferred_element_type=F32)
    out_ref[...] = flipped.astype(BF16).reshape(LINE, PART, BORDERED)


def conv_kernel(core_ref, act_ref, weight_ref, pick_ref, out_ref, before, windows):
    core = core_ref[0]

    @pl.when(core == 1)
    def _():
        before[...] = act_ref[0]

    @pl.when(core == 0)
    def _():
        before[0] = jnp.zeros_like(before[0])
        before[1:] = act_ref[1, : LINE - 1]

    here = act_ref[core].reshape(LINE * PART, BORDERED)
    prior = before[...].reshape(LINE * PART, BORDERED)

    def picked(block, which):
        return jnp.dot(block, pick_ref[which], preferred_element_type=F32)

    for dt in range(3):
        if dt == 0:
            taken = picked(prior, 0)
        elif dt == 1:
            taken = picked(here, 1) + picked(prior, 2)
        else:
            taken = picked(here, 0)
        taken = taken.astype(BF16)
        for tap in range(9):
            for y in range(LINE):
                windows[
                    (9 * dt + tap) * PART : (9 * dt + tap + 1) * PART, y * CELLS : (y + 1) * CELLS
                ] = taken[y * PART : (y + 1) * PART, tap * CELLS : (tap + 1) * CELLS]
    weight = weight_ref[...].reshape(27 * PART, CHANS)
    sums = lax.dot_general(weight, windows[...], TN_DIMS, preferred_element_type=F32)
    for y in range(LINE):
        out_ref[y] = sums[:, y * CELLS : (y + 1) * CELLS].astype(BF16)


def block_kernel(part_ref, lat_ref, bias_ref, out_ref):
    total = part_ref[0].astype(F32)
    for y in range(1, LINE):
        total = total + part_ref[y].astype(F32)
    conv_out = total.T + bias_ref[...]
    block = (lat_ref[...].reshape(CELLS, CHANS).astype(F32) + conv_out).astype(BF16)
    out_ref[...] = block.reshape(FRAMES, ROWS, COLS, CHANS)


def upper_kernel(up_ref, block_ref, down_ref, weight_ref, bias_ref, pick_ref, out_ref):
    pieces = []
    for f in range(FRAMES):
        pieces += [up_ref[f], block_ref[f].reshape(ROWS * COLS, CHANS), down_ref[f]]
    bordered = jnp.concatenate(pieces, axis=0)
    rows = jnp.dot(pick_ref[...], bordered, preferred_element_type=F32).astype(BF16)
    cells = COLS * FRAMES * 2 * ROWS
    total = jnp.zeros((cells, 6 * OUTS), F32)
    for dy in range(3):
        weight = weight_ref[3 * dy : 3 * dy + 3].reshape(6 * OUTS, CHANS)
        total = total + lax.dot_general(
            rows[dy * cells : (dy + 1) * cells], weight, NT_DIMS, preferred_element_type=F32
        )
    wide = 2 * OUTS
    lines = FRAMES * 2 * ROWS
    total = total.reshape(COLS, lines, 3 * wide)
    left = lax.broadcasted_iota(jnp.int32, (lines, wide), 1) < OUTS
    zero = jnp.zeros((lines, wide), F32)
    for c in range(COLS):
        first = total[c, :, :wide]
        first_before = total[c - 1, :, :wide] if c else zero
        last = total[c, :, 2 * wide :]
        last_after = total[c + 1, :, 2 * wide :] if c < COLS - 1 else zero
        value = (
            jnp.where(left, first_before, first)
            + total[c, :, wide : 2 * wide]
            + jnp.where(left, last, last_after)
            + bias_ref[...]
        )
        out_ref[:, c * wide : (c + 1) * wide] = value.astype(BF16)


def row_neighbours(block):
    axes = ("z", "x")
    count = lax.axis_size(axes)
    down = [(i, i + 1) for i in range(count - 1)]
    up = [(i + 1, i) for i in range(count - 1)]
    above = lax.ppermute(block[:, ROWS - 1], axes, down)
    below = lax.ppermute(block[:, 0], axes, up)
    return above, below


def call(kernel, shape, **kwargs):
    return pl.pallas_call(
        kernel, out_shape=jax.ShapeDtypeStruct(shape, BF16), compiler_params=PARAMS, **kwargs
    )


def local(latent, gain_first, conv_first, bias_first, conv_upper, bias_upper):
    above, below = row_neighbours(latent)
    weight = lax.all_gather(conv_first, "core", axis=1, tiled=True)
    upper = jnp.swapaxes(conv_upper, 1, 2)
    upper = jnp.concatenate([upper, upper], axis=1)
    upper_bias = jnp.tile(bias_upper, 2)[None]
    acts = call(act_kernel, (LINE, PART, BORDERED))(above, latent, below, gain_first[None])
    acts = lax.all_to_all(acts, "y", 0, 0, tiled=True)
    acts = lax.all_gather(acts, "core", axis=0, tiled=False)
    core = lax.axis_index("core").astype(jnp.int32)[None]
    vmem = pl.BlockSpec(memory_space=pltpu.VMEM)
    parts = call(
        conv_kernel,
        (LINE, CHANS, CELLS),
        in_specs=[pl.BlockSpec(memory_space=pltpu.SMEM), vmem, vmem, vmem],
        out_specs=vmem,
        scratch_shapes=[
            pltpu.VMEM((LINE, PART, BORDERED), BF16),
            pltpu.VMEM((27 * PART, LINE * CELLS), BF16),
        ],
    )(core, acts, weight, jnp.asarray(window_picks(), BF16))
    parts = lax.all_to_all(parts, "y", 0, 0, tiled=True)
    block = call(block_kernel, (FRAMES, ROWS, COLS, CHANS))(parts, latent, bias_first[None])
    above, below = row_neighbours(block)
    out = call(upper_kernel, (FRAMES * 2 * ROWS, 2 * COLS * OUTS))(
        above, block, below, upper, upper_bias, jnp.asarray(row_picks(), BF16)
    )
    return out.reshape(FRAMES, 2 * ROWS, 2 * COLS * OUTS)


def solution(mesh):
    fine = Mesh(mesh.devices.reshape(8, 2, 8, 4), ("y", "core", "z", "x"))
    tm, rows = ("y", "core"), ("z", "x")
    in_specs = (P(tm, rows, None, None), P(), P(None, tm, None), P(), P(), P())
    return jax.shard_map(
        local, mesh=fine, in_specs=in_specs, out_specs=P(tm, rows, None), check_vma=False
    )
```

```python
import jax
import jax.numpy as jnp
import numpy as np
from jax import lax
from jax.experimental import pallas as pl
from jax.experimental.pallas import tpu as pltpu
from jax.sharding import Mesh
from jax.sharding import PartitionSpec as P

F32 = jnp.float32
BF16 = jnp.bfloat16
FRAMES, ROWS, COLS, CHANS, OUTS = 2, 4, 16, 384, 192
LINE = 8
PART = CHANS // LINE
PAIRS = LINE // 2
HALF = ROWS // 2
CELLS = FRAMES * HALF * COLS
SENT = FRAMES * (HALF + 2) * COLS
BORDERED = FRAMES * (ROWS + 2) * COLS
NT_DIMS = (((1,), (1,)), ((), ()))
TN_DIMS = (((0,), (0,)), ((), ()))
PARAMS = pltpu.CompilerParams(vmem_limit_bytes=40 * 1024 * 1024)


def window_picks():
    picks = np.zeros((3, 2, FRAMES, HALF + 2, COLS, 9, 2, FRAMES, HALF, COLS), np.float32)
    for dy in range(3):
        for dx in range(3):
            for r in range(HALF):
                for c in range(COLS):
                    col = c + dx - 1
                    if 0 <= col < COLS:
                        for p in range(2):
                            for f in range(FRAMES):
                                tap = 3 * dy + dx
                                picks[0, p, f, r + dy, col, tap, p, f, r, c] = 1
                                which = 1 if f == 0 else 2
                                picks[which, p, f, r + dy, col, tap, p, 1 - f, r, c] = 1
    return picks.reshape(3, 2 * SENT, 9 * 2 * CELLS)


def row_picks():
    picks = np.zeros((3, COLS, FRAMES, 2 * ROWS, FRAMES, ROWS + 2, COLS), np.float32)
    for dy in range(3):
        for i in range(2 * ROWS):
            row = (i + dy - 1) // 2 + 1
            for f in range(FRAMES):
                for c in range(COLS):
                    picks[dy, c, f, i, f, row, c] = 1
    return picks.reshape(3 * COLS * FRAMES * 2 * ROWS, BORDERED)


def act_kernel(up_ref, lat_ref, down_ref, gain_ref, out_ref):
    pieces = []
    for f in range(FRAMES):
        pieces += [up_ref[f], lat_ref[f].reshape(ROWS * COLS, CHANS), down_ref[f]]
    values = jnp.concatenate(pieces, axis=0).astype(F32)
    mean_square = jnp.mean(values * values, axis=-1, keepdims=True)
    scaled = values * lax.rsqrt(mean_square + 1e-06) * gain_ref[...].reshape(1, CHANS)
    act = (scaled / (1.0 + jnp.exp(-scaled))).astype(BF16)
    row = lax.broadcasted_iota(jnp.int32, (CHANS, CHANS), 0)
    col = lax.broadcasted_iota(jnp.int32, (CHANS, CHANS), 1)
    eye = jnp.where(row == col, 1.0, 0.0).astype(BF16)
    for half in range(2):
        cells = []
        for f in range(FRAMES):
            start = (f * (ROWS + 2) + half * HALF) * COLS
            cells.append(act[start : start + (HALF + 2) * COLS])
        flipped = lax.dot_general(
            eye, jnp.concatenate(cells, axis=0), NT_DIMS, preferred_element_type=F32
        )
        flipped = flipped.astype(BF16).reshape(PAIRS, 2 * PART, SENT)
        for pair in range(PAIRS):
            out_ref[2 * pair + half] = flipped[pair]


def conv_kernel(
    place_ref, act_ref, own_ref, other_ref, pick_ref, out_ref, here, before, windows
):
    core, half = place_ref[0], place_ref[1]
    for y in range(LINE):
        where = (y // 2, slice(None), slice((y % 2) * SENT, (y % 2 + 1) * SENT))
        here[where] = act_ref[core, y]

        @pl.when(core == 1)
        def _():
            before[where] = act_ref[0, y]

        @pl.when(core == 0)
        def _():
            before[where] = act_ref[1, y - 1] if y else jnp.zeros_like(act_ref[1, 0])

    now = here[...].reshape(PAIRS * 2 * PART, 2 * SENT)
    prior = before[...].reshape(PAIRS * 2 * PART, 2 * SENT)

    def picked(block, which):
        return jnp.dot(block, pick_ref[which], preferred_element_type=F32)

    lanes = 2 * CELLS
    for dt in range(3):
        if dt == 0:
            taken = picked(prior, 0)
        elif dt == 1:
            taken = picked(now, 1) + picked(prior, 2)
        else:
            taken = picked(now, 0)
        taken = taken.astype(BF16)
        for tap in range(9):
            for pair in range(PAIRS):
                for part in range(2):
                    row = (2 * pair + part) * PART
                    windows[
                        part,
                        (9 * dt + tap) * PART : (9 * dt + tap + 1) * PART,
                        pair * lanes : (pair + 1) * lanes,
                    ] = taken[row : row + PART, tap * lanes : (tap + 1) * lanes]
    sums = lax.dot_general(
        windows[half],
        own_ref[...].reshape(27 * PART, CHANS),
        TN_DIMS,
        preferred_element_type=F32,
    )
    sums = sums + lax.dot_general(
        windows[1 - half],
        other_ref[...].reshape(27 * PART, CHANS),
        TN_DIMS,
        preferred_element_type=F32,
    )
    out_ref[...] = sums.astype(BF16).reshape(LINE, CELLS, CHANS)


def block_kernel(part_ref, lat_ref, bias_ref, out_ref):
    bias = bias_ref[...].reshape(1, CHANS)
    for half in range(2):
        total = part_ref[half].astype(F32)
        for y in range(half + 2, LINE, 2):
            total = total + part_ref[y].astype(F32)
        total = total + bias
        size = HALF * COLS
        for f in range(FRAMES):
            rows = slice(half * HALF, (half + 1) * HALF)
            skip = lat_ref[f, rows].reshape(size, CHANS).astype(F32)
            value = (skip + total[f * size : (f + 1) * size]).astype(BF16)
            out_ref[f, rows] = value.reshape(HALF, COLS, CHANS)


def upper_kernel(up_ref, block_ref, down_ref, weight_ref, bias_ref, pick_ref, out_ref):
    pieces = []
    for f in range(FRAMES):
        pieces += [up_ref[f], block_ref[f].reshape(ROWS * COLS, CHANS), down_ref[f]]
    bordered = jnp.concatenate(pieces, axis=0)
    rows = jnp.dot(pick_ref[...], bordered, preferred_element_type=F32).astype(BF16)
    cells = COLS * FRAMES * 2 * ROWS
    total = jnp.zeros((cells, 6 * OUTS), F32)
    for dy in range(3):
        weight = weight_ref[3 * dy : 3 * dy + 3].reshape(6 * OUTS, CHANS)
        total = total + lax.dot_general(
            rows[dy * cells : (dy + 1) * cells], weight, NT_DIMS, preferred_element_type=F32
        )
    wide = 2 * OUTS
    lines = FRAMES * 2 * ROWS
    total = total.reshape(COLS, lines, 3 * wide)
    left = lax.broadcasted_iota(jnp.int32, (lines, wide), 1) < OUTS
    zero = jnp.zeros((lines, wide), F32)
    for c in range(COLS):
        first = total[c, :, :wide]
        first_before = total[c - 1, :, :wide] if c else zero
        last = total[c, :, 2 * wide :]
        last_after = total[c + 1, :, 2 * wide :] if c < COLS - 1 else zero
        value = (
            jnp.where(left, first_before, first)
            + total[c, :, wide : 2 * wide]
            + jnp.where(left, last, last_after)
            + bias_ref[...]
        )
        out_ref[:, c * wide : (c + 1) * wide] = value.astype(BF16)


def row_neighbours(block):
    axes = ("z", "x")
    count = lax.axis_size(axes)
    down = [(i, i + 1) for i in range(count - 1)]
    up = [(i + 1, i) for i in range(count - 1)]
    above = lax.ppermute(block[:, ROWS - 1], axes, down)
    below = lax.ppermute(block[:, 0], axes, up)
    return above, below


def call(kernel, shape, **kwargs):
    return pl.pallas_call(
        kernel, out_shape=jax.ShapeDtypeStruct(shape, BF16), compiler_params=PARAMS, **kwargs
    )


def local(latent, gain_first, conv_first, bias_first, conv_upper, bias_upper):
    other = lax.ppermute(conv_first, "y", [(i, i ^ 1) for i in range(LINE)])
    above, below = row_neighbours(latent)
    own = lax.all_gather(conv_first, "core", axis=1, tiled=True)
    other = lax.all_gather(other, "core", axis=1, tiled=True)
    upper = jnp.swapaxes(conv_upper, 1, 2)
    upper = jnp.concatenate([upper, upper], axis=1)
    upper_bias = jnp.tile(bias_upper, 2)[None]
    acts = call(act_kernel, (LINE, 2 * PART, SENT))(above, latent, below, gain_first)
    acts = lax.all_to_all(acts, "y", 0, 0, tiled=True)
    acts, own, other, upper, upper_bias = lax.optimization_barrier(
        (acts, own, other, upper, upper_bias)
    )
    acts = lax.all_gather(acts, "core", axis=0, tiled=False)
    place = jnp.stack([lax.axis_index("core"), lax.axis_index("y") % 2]).astype(jnp.int32)
    vmem = pl.BlockSpec(memory_space=pltpu.VMEM)
    parts = call(
        conv_kernel,
        (LINE, CELLS, CHANS),
        in_specs=[pl.BlockSpec(memory_space=pltpu.SMEM), vmem, vmem, vmem, vmem],
        out_specs=vmem,
        scratch_shapes=[
            pltpu.VMEM((PAIRS, 2 * PART, 2 * SENT), BF16),
            pltpu.VMEM((PAIRS, 2 * PART, 2 * SENT), BF16),
            pltpu.VMEM((2, 27 * PART, LINE * CELLS), BF16),
        ],
    )(place, acts, own, other, jnp.asarray(window_picks(), BF16))
    parts = lax.all_to_all(parts, "y", 0, 0, tiled=True)
    block = call(block_kernel, (FRAMES, ROWS, COLS, CHANS))(parts, latent, bias_first)
    above, below = row_neighbours(block)
    out = call(upper_kernel, (FRAMES * 2 * ROWS, 2 * COLS * OUTS))(
        above, block, below, upper, upper_bias, jnp.asarray(row_picks(), BF16)
    )
    return out.reshape(FRAMES, 2 * ROWS, 2 * COLS * OUTS)


def solution(mesh):
    fine = Mesh(mesh.devices.reshape(8, 2, 8, 4), ("y", "core", "z", "x"))
    tm, rows = ("y", "core"), ("z", "x")
    in_specs = (P(tm, rows, None, None), P(), P(None, tm, None), P(), P(), P())
    return jax.shard_map(
        local, mesh=fine, in_specs=in_specs, out_specs=P(tm, rows, None), check_vma=False
    )
```

```python
import jax
import jax.numpy as jnp
from jax import lax
from jax.experimental import pallas as pl
from jax.experimental.pallas import tpu as pltpu
from jax.sharding import Mesh
from jax.sharding import PartitionSpec as P

F32 = jnp.float32
BF16 = jnp.bfloat16
FRAMES, ROWS, COLS, CHANS, OUTS = 2, 4, 16, 384, 192
LINE = 8
PART = CHANS // LINE
PAIRS = LINE // 2
HALF = ROWS // 2
CELLS = FRAMES * HALF * COLS
SENT = FRAMES * ROWS * COLS
EDGE = LINE * FRAMES * COLS
BORDERED = FRAMES * (ROWS + 2) * COLS
NT_DIMS = (((1,), (1,)), ((), ()))
TN_DIMS = (((0,), (0,)), ((), ()))


def one_hot(wanted, there):
    return jnp.where(wanted == there, 1.0, 0.0).astype(BF16)


def window_picks(half):
    lane = lax.broadcasted_iota(jnp.int32, (1, 18 * CELLS), 1)
    tap, frame, row, col = lane >> 7, (lane >> 5) & 3, (lane >> 4) & 1, lane & 15
    dy = (tap * 11) >> 5
    col = col + tap - 3 * dy - 1
    row = row + dy - 1 + 2 * half
    wanted = (frame << 6) + (row << 4) + col
    inside = (col >= 0) & (col < COLS) & (row >= 0) & (row < ROWS)
    wanted = jnp.where(inside, wanted, -1)
    return one_hot(wanted, lax.broadcasted_iota(jnp.int32, (2 * SENT, 18 * CELLS), 0))


def edge_picks(shift):
    lane = lax.broadcasted_iota(jnp.int32, (1, 3 * EDGE), 1)
    col = (lane & 15) + (lane >> 8) - 1
    wanted = (((lane >> 4) & 15) << 4) + col - shift
    wanted = jnp.where((col >= 0) & (col < COLS), wanted, -1)
    return one_hot(wanted, lax.broadcasted_iota(jnp.int32, (EDGE, 3 * EDGE), 0))


def row_picks():
    shape = (6 * ROWS * COLS * FRAMES, BORDERED)
    place = lax.broadcasted_iota(jnp.int32, (shape[0], 1), 0)
    dy, col, frame, i = place >> 8, (place >> 4) & 15, (place >> 3) & 1, place & 7
    wanted = frame * ((ROWS + 2) * COLS) + (((i + dy + 1) >> 1) << 4) + col
    return one_hot(wanted, lax.broadcasted_iota(jnp.int32, shape, 1))


def scaled_silu(block, gain):
    values = block.astype(F32)
    mean_square = jnp.mean(values * values, axis=-1, keepdims=True)
    scaled = values * lax.rsqrt(mean_square + 1e-06) * gain
    return (scaled / (1.0 + jnp.exp(-scaled))).astype(BF16)


def act_kernel(lat_ref, gain_ref, out_ref, lat, gain, arrived):
    copies = [
        pltpu.make_async_copy(lat_ref, lat, arrived.at[0]),
        pltpu.make_async_copy(gain_ref, gain, arrived.at[1]),
    ]
    for copy in copies:
        copy.start()
    row = lax.broadcasted_iota(jnp.int32, (CHANS, CHANS), 0)
    col = lax.broadcasted_iota(jnp.int32, (CHANS, CHANS), 1)
    eye = one_hot(row, col)
    for copy in copies:
        copy.wait()
    act = scaled_silu(lat[...].reshape(SENT, CHANS), gain[...].reshape(1, CHANS))
    flipped = lax.dot_general(eye, act, NT_DIMS, preferred_element_type=F32).astype(BF16)
    for y in range(LINE):
        start = (y // 2) * 2 * PART
        out_ref[y] = flipped[start : start + 2 * PART]


def pack_kernel(act_ref, out_ref):
    row = (ROWS - 1) * (1 - (lax.axis_index("y") & 1))
    lane = lax.broadcasted_iota(jnp.int32, (1, SENT), 1)
    wanted = ((lane >> 4) << 6) + (row << 4) + (lane & 15)
    picks = one_hot(wanted, lax.broadcasted_iota(jnp.int32, (4 * SENT, SENT), 0))
    for core in range(2):
        for group in range(2):
            block = jnp.concatenate([act_ref[core, 4 * group + k] for k in range(4)], axis=1)
            packed = jnp.dot(block, picks, preferred_element_type=F32)
            out_ref[core, group] = packed.astype(BF16)


def weight_dots(blocks, weights, half):
    total = None
    for i in range(2):
        rows = blocks.shape[1]
        part = lax.dot_general(
            blocks[half if i == 0 else 1 - half],
            weights[i].reshape(rows, CHANS),
            TN_DIMS,
            preferred_element_type=F32,
        )
        total = part if total is None else total + part
    return total


def inner_kernel(act_ref, own_ref, other_ref, out_ref, here, before, windows, weights, arrived):
    core, half = lax.axis_index("core"), lax.axis_index("y") & 1
    copies = [
        pltpu.make_async_copy(ref, weights.at[i], arrived.at[i])
        for i, ref in enumerate((own_ref, other_ref))
    ]
    for copy in copies:
        copy.start()
    for y in range(LINE):
        where = (y // 2, slice(None), slice((y % 2) * SENT, (y % 2 + 1) * SENT))
        here[where] = act_ref[core, y]

        @pl.when(core == 1)
        def _():
            before[where] = act_ref[0, y]

        @pl.when(core == 0)
        def _():
            before[where] = act_ref[1, y - 1] if y else jnp.zeros_like(act_ref[1, 0])

    now = here[...].reshape(PAIRS * 2 * PART, 2 * SENT)
    prior = before[...].reshape(PAIRS * 2 * PART, 2 * SENT)
    picks = window_picks(half)
    earliest = jnp.dot(prior, picks, preferred_element_type=F32)
    latest = jnp.dot(now, picks, preferred_element_type=F32)
    lanes = 2 * CELLS
    step = lanes // 4
    frame = (lax.broadcasted_iota(jnp.int32, (PAIRS * 2 * PART, lanes), 1) >> 5) & 1
    for tap in range(9):
        first = earliest[:, tap * lanes : (tap + 1) * lanes]
        last = latest[:, tap * lanes : (tap + 1) * lanes]
        middle = jnp.where(
            frame == 0, pltpu.roll(first, lanes - step, 1), pltpu.roll(last, step, 1)
        )
        for dt, taken in enumerate((first, middle, last)):
            taken = taken.astype(BF16)
            for pair in range(PAIRS):
                for part in range(2):
                    row = (2 * pair + part) * PART
                    windows[
                        part,
                        (9 * dt + tap) * PART : (9 * dt + tap + 1) * PART,
                        pair * lanes : (pair + 1) * lanes,
                    ] = taken[row : row + PART]
    for copy in copies:
        copy.wait()
    sums = weight_dots(windows, weights, half)
    out_ref[...] = sums.reshape(out_ref.shape)


def edge_kernel(edge_ref, part_ref, own_ref, other_ref, out_ref, windows, weights, arrived):
    core, half = lax.axis_index("core"), lax.axis_index("y") & 1
    copies = []
    for i, ref in enumerate((own_ref, other_ref)):
        for dt in range(3):
            taps = ref.at[pl.ds(9 * dt + 6 * half, 3)]
            copies.append(pltpu.make_async_copy(taps, weights.at[i, dt], arrived.at[i, dt]))
    for copy in copies:
        copy.start()

    def windows_of(which, shift):
        block = jnp.concatenate([edge_ref[which, 0], edge_ref[which, 1]], axis=1)
        return jnp.dot(block, edge_picks(shift), preferred_element_type=F32)

    earliest = windows_of(1 - core, 2 * COLS * (1 - core))
    latest = windows_of(core, 0)
    frame = (lax.broadcasted_iota(jnp.int32, (2 * PART, EDGE), 1) >> 4) & 1
    for dx in range(3):
        first = earliest[:, dx * EDGE : (dx + 1) * EDGE]
        last = latest[:, dx * EDGE : (dx + 1) * EDGE]
        middle = jnp.where(
            frame == 0, pltpu.roll(first, EDGE - COLS, 1), pltpu.roll(last, COLS, 1)
        )
        for dt, taken in enumerate((first, middle, last)):
            taken = taken.astype(BF16)
            for part in range(2):
                row = (3 * dt + dx) * PART
                windows[part, row : row + PART] = taken[part * PART : (part + 1) * PART]
    for copy in copies:
        copy.wait()
    sums = weight_dots(windows, weights, half)
    for y in range(LINE):
        for f in range(FRAMES):
            beside = sums[(2 * y + f) * COLS : (2 * y + f + 1) * COLS]
            for r in range(HALF):
                value = part_ref[y, f, r] + jnp.where(half == r, beside, 0.0)
                row = (f * HALF + r) * COLS
                out_ref[y, row : row + COLS] = value.astype(BF16)


def block_kernel(part_ref, lat_ref, bias_ref, later_ref, out_ref):
    del later_ref
    bias = bias_ref[...].reshape(1, CHANS)
    for half in range(2):
        total = part_ref[half].astype(F32)
        for y in range(half + 2, LINE, 2):
            total = total + part_ref[y].astype(F32)
        total = total + bias
        size = HALF * COLS
        for f in range(FRAMES):
            rows = slice(half * HALF, (half + 1) * HALF)
            skip = lat_ref[f, rows].reshape(size, CHANS).astype(F32)
            value = (skip + total[f * size : (f + 1) * size]).astype(BF16)
            out_ref[f, rows] = value.reshape(HALF, COLS, CHANS)


def upper_kernel(up_ref, block_ref, down_ref, weight_ref, bias_ref, out_ref):
    pieces = []
    for f in range(FRAMES):
        pieces += [up_ref[f], block_ref[f].reshape(ROWS * COLS, CHANS), down_ref[f]]
    bordered = jnp.concatenate(pieces, axis=0)
    rows = jnp.dot(row_picks(), bordered, preferred_element_type=F32).astype(BF16)
    cells = COLS * FRAMES * 2 * ROWS
    total = jnp.zeros((cells, 6 * OUTS), F32)
    for dy in range(3):
        weight = weight_ref[3 * dy : 3 * dy + 3].reshape(6 * OUTS, CHANS)
        total = total + lax.dot_general(
            rows[dy * cells : (dy + 1) * cells], weight, NT_DIMS, preferred_element_type=F32
        )
    wide = 2 * OUTS
    bias = bias_ref[...].reshape(1, OUTS)
    bias = jnp.concatenate([bias, bias], axis=1)
    lines = FRAMES * 2 * ROWS
    total = total.reshape(COLS, lines, 3 * wide)
    left = lax.broadcasted_iota(jnp.int32, (lines, wide), 1) < OUTS
    zero = jnp.zeros((lines, wide), F32)
    for c in range(COLS):
        first = total[c, :, :wide]
        first_before = total[c - 1, :, :wide] if c else zero
        last = total[c, :, 2 * wide :]
        last_after = total[c + 1, :, 2 * wide :] if c < COLS - 1 else zero
        value = (
            jnp.where(left, first_before, first)
            + total[c, :, wide : 2 * wide]
            + jnp.where(left, last, last_after)
            + bias
        )
        out_ref[:, c * wide : (c + 1) * wide] = value.astype(BF16)


def row_neighbours(block):
    axes = ("z", "x")
    count = lax.axis_size(axes)
    down = [(i, i + 1) for i in range(count - 1)]
    up = [(i + 1, i) for i in range(count - 1)]
    above = lax.ppermute(block[:, ROWS - 1], axes, down)
    below = lax.ppermute(block[:, 0], axes, up)
    return above, below


def row_beside(edges):
    axes = ("y", "z", "x")
    count = lax.axis_size(("z", "x"))
    pairs = []
    for y in range(LINE):
        for i in range(count):
            j = i + 1 if y % 2 == 0 else i - 1
            if 0 <= j < count:
                pairs.append((y * count + i, y * count + j))
    return lax.ppermute(edges, axes, pairs)


def call(kernel, shape, inputs, scratch=(), kind=BF16, limit=16):
    spaces = [pltpu.HBM if far else pltpu.VMEM for _, far in inputs]
    return pl.pallas_call(
        kernel,
        out_shape=jax.ShapeDtypeStruct(shape, kind),
        in_specs=[pl.BlockSpec(memory_space=space) for space in spaces],
        out_specs=pl.BlockSpec(memory_space=pltpu.VMEM),
        scratch_shapes=list(scratch),
        compiler_params=pltpu.CompilerParams(vmem_limit_bytes=limit * 1024 * 1024),
    )(*[array for array, _ in inputs])


def local(latent, gain_first, conv_first, bias_first, conv_upper, bias_upper):
    other = lax.ppermute(conv_first, "y", [(i, i ^ 1) for i in range(LINE)])
    acts = call(
        act_kernel,
        (LINE, 2 * PART, SENT),
        [(latent, True), (gain_first, True)],
        [
            pltpu.VMEM(latent.shape, BF16),
            pltpu.VMEM(gain_first.shape, F32),
            pltpu.SemaphoreType.DMA((2,)),
        ],
    )
    acts, conv_first, conv_upper = lax.optimization_barrier((acts, conv_first, conv_upper))
    own = lax.all_gather(conv_first, "core", axis=1, tiled=True)
    other = lax.all_gather(other, "core", axis=1, tiled=True)
    upper = jnp.swapaxes(conv_upper, 1, 2)
    upper = jnp.concatenate([upper, upper], axis=1)
    acts = lax.all_to_all(acts, "y", 0, 0, tiled=True)
    acts, own, other = lax.optimization_barrier((acts, own, other))
    acts = lax.all_gather(acts, "core", axis=0, tiled=False)
    edges = row_beside(call(pack_kernel, (2, 2, 2 * PART, SENT), [(acts, False)]))
    parts = call(
        inner_kernel,
        (LINE, FRAMES, HALF, COLS, CHANS),
        [(acts, False), (own, True), (other, True)],
        [
            pltpu.VMEM((PAIRS, 2 * PART, 2 * SENT), BF16),
            pltpu.VMEM((PAIRS, 2 * PART, 2 * SENT), BF16),
            pltpu.VMEM((2, 27 * PART, LINE * CELLS), BF16),
            pltpu.VMEM((2, 27, PART, CHANS), BF16),
            pltpu.SemaphoreType.DMA((2,)),
        ],
        kind=F32,
        limit=32,
    )
    parts = call(
        edge_kernel,
        (LINE, CELLS, CHANS),
        [(edges, False), (parts, False), (own, True), (other, True)],
        [
            pltpu.VMEM((2, 9 * PART, EDGE), BF16),
            pltpu.VMEM((2, 3, 3, PART, CHANS), BF16),
            pltpu.SemaphoreType.DMA((2, 3)),
        ],
    )
    parts = lax.all_to_all(parts, "y", 0, 0, tiled=True)
    block = call(
        block_kernel,
        (FRAMES, ROWS, COLS, CHANS),
        [(parts, False), (latent, False), (bias_first, False), (upper, True)],
    )
    above, below = row_neighbours(block)
    out = call(
        upper_kernel,
        (FRAMES * 2 * ROWS, 2 * COLS * OUTS),
        [(array, False) for array in (above, block, below, upper, bias_upper)],
    )
    return out.reshape(FRAMES, 2 * ROWS, 2 * COLS * OUTS)


def solution(mesh):
    fine = Mesh(mesh.devices.reshape(8, 2, 8, 4), ("y", "core", "z", "x"))
    tm, rows = ("y", "core"), ("z", "x")
    in_specs = (P(tm, rows, None, None), P(), P(None, tm, None), P(), P(), P())
    return jax.shard_map(
        local, mesh=fine, in_specs=in_specs, out_specs=P(tm, rows, None), check_vma=False
    )
```

```python
import jax
import jax.numpy as jnp
from jax import lax
from jax.experimental import pallas as pl
from jax.experimental.pallas import tpu as pltpu
from jax.sharding import Mesh
from jax.sharding import PartitionSpec as P

F32 = jnp.float32
BF16 = jnp.bfloat16
FRAMES, ROWS, COLS, CHANS, OUTS = 2, 4, 16, 384, 192
LINE = 8
PART = CHANS // LINE
PAIRS = LINE // 2
HALF = ROWS // 2
CELLS = FRAMES * HALF * COLS
SENT = FRAMES * ROWS * COLS
EDGE = LINE * FRAMES * COLS
ORDER = (4, 5, 6, 7, 0, 1, 2, 3)
SLOT = tuple(ORDER.index(y) for y in range(LINE))
NT_DIMS = (((1,), (1,)), ((), ()))
TN_DIMS = (((0,), (0,)), ((), ()))


def one_hot(wanted, there):
    return jnp.where(wanted == there, 1.0, 0.0).astype(BF16)


def window_picks(half):
    lane = lax.broadcasted_iota(jnp.int32, (1, 18 * CELLS), 1)
    tap, frame, row, col = lane >> 7, (lane >> 5) & 3, (lane >> 4) & 1, lane & 15
    dy = (tap * 11) >> 5
    col = col + tap - 3 * dy - 1
    row = row + dy - 1 + 2 * half
    wanted = (frame << 6) + (row << 4) + col
    inside = (col >= 0) & (col < COLS) & (row >= 0) & (row < ROWS)
    wanted = jnp.where(inside, wanted, -1)
    return one_hot(wanted, lax.broadcasted_iota(jnp.int32, (2 * SENT, 18 * CELLS), 0))


def edge_picks(shift):
    lane = lax.broadcasted_iota(jnp.int32, (1, 3 * EDGE), 1)
    col = (lane & 15) + (lane >> 8) - 1
    wanted = (((lane >> 4) & 15) << 4) + col - shift
    wanted = jnp.where((col >= 0) & (col < COLS), wanted, -1)
    return one_hot(wanted, lax.broadcasted_iota(jnp.int32, (EDGE, 3 * EDGE), 0))


def row_picks():
    shape = (6 * ROWS * COLS * FRAMES, SENT)
    place = lax.broadcasted_iota(jnp.int32, (shape[0], 1), 0)
    dy, col, frame, i = place >> 8, (place >> 4) & 15, (place >> 3) & 1, place & 7
    row = ((i + dy + 1) >> 1) - 1
    wanted = (frame << 6) + (row << 4) + col
    wanted = jnp.where((row >= 0) & (row < ROWS), wanted, -1)
    return one_hot(wanted, lax.broadcasted_iota(jnp.int32, shape, 1))


def scaled_silu(block, gain):
    values = block.astype(F32)
    mean_square = jnp.mean(values * values, axis=-1, keepdims=True)
    scaled = values * lax.rsqrt(mean_square + 1e-06) * gain
    return (scaled / (1.0 + jnp.exp(-scaled))).astype(BF16)


def act_kernel(lat_ref, gain_ref, out_ref, lat, gain, arrived):
    copies = [
        pltpu.make_async_copy(lat_ref, lat, arrived.at[0]),
        pltpu.make_async_copy(gain_ref, gain, arrived.at[1]),
    ]
    for copy in copies:
        copy.start()
    row = lax.broadcasted_iota(jnp.int32, (CHANS, CHANS), 0)
    col = lax.broadcasted_iota(jnp.int32, (CHANS, CHANS), 1)
    eye = one_hot(row, col)
    for copy in copies:
        copy.wait()
    act = scaled_silu(lat[...].reshape(SENT, CHANS), gain[...].reshape(1, CHANS))
    flipped = lax.dot_general(eye, act, NT_DIMS, preferred_element_type=F32).astype(BF16)
    for y in range(LINE):
        start = (y // 2) * 2 * PART
        out_ref[SLOT[y]] = flipped[start : start + 2 * PART]


def pack_kernel(act_ref, out_ref):
    row = (ROWS - 1) * (1 - (lax.axis_index("y") & 1))
    lane = lax.broadcasted_iota(jnp.int32, (1, SENT), 1)
    wanted = ((lane >> 4) << 6) + (row << 4) + (lane & 15)
    picks = one_hot(wanted, lax.broadcasted_iota(jnp.int32, (4 * SENT, SENT), 0))
    for core in range(2):
        for group in range(2):
            block = jnp.concatenate([act_ref[core, SLOT[4 * group + k]] for k in range(4)], axis=1)
            packed = jnp.dot(block, picks, preferred_element_type=F32)
            out_ref[core, group] = packed.astype(BF16)


def weight_dots(blocks, weights, half):
    total = None
    for i in range(2):
        rows = blocks.shape[1]
        part = lax.dot_general(
            blocks[half if i == 0 else 1 - half],
            weights[i].reshape(rows, CHANS),
            TN_DIMS,
            preferred_element_type=F32,
        )
        total = part if total is None else total + part
    return total


def inner_kernel(act_ref, own_ref, other_ref, out_ref, here, before, windows, weights, arrived):
    core, half = lax.axis_index("core"), lax.axis_index("y") & 1
    copies = [
        pltpu.make_async_copy(ref, weights.at[i], arrived.at[i])
        for i, ref in enumerate((own_ref, other_ref))
    ]
    for copy in copies:
        copy.start()
    for y in range(LINE):
        where = (y // 2, slice(None), slice((y % 2) * SENT, (y % 2 + 1) * SENT))
        here[where] = act_ref[core, SLOT[y]]

        @pl.when(core == 1)
        def _():
            before[where] = act_ref[0, SLOT[y]]

        @pl.when(core == 0)
        def _():
            before[where] = act_ref[1, SLOT[y - 1]] if y else jnp.zeros_like(act_ref[1, 0])

    now = here[...].reshape(PAIRS * 2 * PART, 2 * SENT)
    prior = before[...].reshape(PAIRS * 2 * PART, 2 * SENT)
    picks = window_picks(half)
    earliest = jnp.dot(prior, picks, preferred_element_type=F32)
    latest = jnp.dot(now, picks, preferred_element_type=F32)
    lanes = 2 * CELLS
    step = lanes // 4
    frame = (lax.broadcasted_iota(jnp.int32, (PAIRS * 2 * PART, lanes), 1) >> 5) & 1
    for tap in range(9):
        first = earliest[:, tap * lanes : (tap + 1) * lanes]
        last = latest[:, tap * lanes : (tap + 1) * lanes]
        middle = jnp.where(
            frame == 0, pltpu.roll(first, lanes - step, 1), pltpu.roll(last, step, 1)
        )
        for dt, taken in enumerate((first, middle, last)):
            taken = taken.astype(BF16)
            for pair in range(PAIRS):
                for part in range(2):
                    row = (2 * pair + part) * PART
                    windows[
                        part,
                        (9 * dt + tap) * PART : (9 * dt + tap + 1) * PART,
                        pair * lanes : (pair + 1) * lanes,
                    ] = taken[row : row + PART]
    for copy in copies:
        copy.wait()
    sums = weight_dots(windows, weights, half)
    out_ref[...] = sums.reshape(out_ref.shape)


def edge_kernel(edge_ref, part_ref, own_ref, other_ref, out_ref, windows, weights, arrived):
    core, half = lax.axis_index("core"), lax.axis_index("y") & 1
    copies = []
    for i, ref in enumerate((own_ref, other_ref)):
        for dt in range(3):
            taps = ref.at[pl.ds(9 * dt + 6 * half, 3)]
            copies.append(pltpu.make_async_copy(taps, weights.at[i, dt], arrived.at[i, dt]))
    for copy in copies:
        copy.start()

    def windows_of(which, shift):
        block = jnp.concatenate([edge_ref[which, 0], edge_ref[which, 1]], axis=1)
        return jnp.dot(block, edge_picks(shift), preferred_element_type=F32)

    earliest = windows_of(1 - core, 2 * COLS * (1 - core))
    latest = windows_of(core, 0)
    frame = (lax.broadcasted_iota(jnp.int32, (2 * PART, EDGE), 1) >> 4) & 1
    for dx in range(3):
        first = earliest[:, dx * EDGE : (dx + 1) * EDGE]
        last = latest[:, dx * EDGE : (dx + 1) * EDGE]
        middle = jnp.where(
            frame == 0, pltpu.roll(first, EDGE - COLS, 1), pltpu.roll(last, COLS, 1)
        )
        for dt, taken in enumerate((first, middle, last)):
            taken = taken.astype(BF16)
            for part in range(2):
                row = (3 * dt + dx) * PART
                windows[part, row : row + PART] = taken[part * PART : (part + 1) * PART]
    for copy in copies:
        copy.wait()
    sums = weight_dots(windows, weights, half)
    for y in range(LINE):
        for f in range(FRAMES):
            beside = sums[(2 * y + f) * COLS : (2 * y + f + 1) * COLS]
            for r in range(HALF):
                value = part_ref[y, f, r] + jnp.where(half == r, beside, 0.0)
                row = (f * HALF + r) * COLS
                out_ref[SLOT[y], row : row + COLS] = value.astype(BF16)


def block_kernel(part_ref, lat_ref, bias_ref, later_ref, out_ref):
    del later_ref
    bias = bias_ref[...].reshape(1, CHANS)
    for half in range(2):
        total = part_ref[SLOT[half]].astype(F32)
        for y in range(half + 2, LINE, 2):
            total = total + part_ref[SLOT[y]].astype(F32)
        total = total + bias
        size = HALF * COLS
        for f in range(FRAMES):
            rows = slice(half * HALF, (half + 1) * HALF)
            skip = lat_ref[f, rows].reshape(size, CHANS).astype(F32)
            value = (skip + total[f * size : (f + 1) * size]).astype(BF16)
            out_ref[f, rows] = value.reshape(HALF, COLS, CHANS)


def upper_inner_kernel(block_ref, weight_ref, out_ref):
    rows = jnp.dot(
        row_picks(), block_ref[...].reshape(SENT, CHANS), preferred_element_type=F32
    ).astype(BF16)
    cells = COLS * FRAMES * 2 * ROWS
    total = None
    for dy in range(3):
        part = lax.dot_general(
            rows[dy * cells : (dy + 1) * cells],
            weight_ref[3 * dy : 3 * dy + 3].reshape(6 * OUTS, CHANS),
            NT_DIMS,
            preferred_element_type=F32,
        )
        total = part if total is None else total + part
    out_ref[...] = total.reshape(out_ref.shape)


def upper_kernel(up_ref, down_ref, inner_ref, weight_ref, bias_ref, out_ref):
    wide = 2 * OUTS
    lines = FRAMES * 2 * ROWS

    def taps(ref, dy):
        return lax.dot_general(
            ref[...].reshape(FRAMES * COLS, CHANS),
            weight_ref[3 * dy : 3 * dy + 3].reshape(3 * wide, CHANS),
            NT_DIMS,
            preferred_element_type=F32,
        )

    above, below = taps(up_ref, 0), taps(down_ref, 2)
    line = lax.broadcasted_iota(jnp.int32, (lines, 3 * wide), 0)
    totals = []
    for c in range(COLS):
        total = inner_ref[c]
        for f in range(FRAMES):
            row = f * COLS + c
            top, bottom = f * 2 * ROWS, (f + 1) * 2 * ROWS - 1
            total = total + jnp.where(line == top, above[row : row + 1], 0.0)
            total = total + jnp.where(line == bottom, below[row : row + 1], 0.0)
        totals.append(total)
    bias = bias_ref[...].reshape(1, OUTS)
    bias = jnp.concatenate([bias, bias], axis=1)
    left = lax.broadcasted_iota(jnp.int32, (lines, wide), 1) < OUTS
    zero = jnp.zeros((lines, wide), F32)
    for c in range(COLS):
        first_before = totals[c - 1][:, :wide] if c else zero
        last_after = totals[c + 1][:, 2 * wide :] if c < COLS - 1 else zero
        value = (
            jnp.where(left, first_before, totals[c][:, :wide])
            + totals[c][:, wide : 2 * wide]
            + jnp.where(left, totals[c][:, 2 * wide :], last_after)
            + bias
        )
        out_ref[:, c * wide : (c + 1) * wide] = value.astype(BF16)


def row_neighbours(block):
    axes = ("z", "x")
    count = lax.axis_size(axes)
    down = [(i, i + 1) for i in range(count - 1)]
    up = [(i + 1, i) for i in range(count - 1)]
    above = lax.ppermute(block[:, ROWS - 1], axes, down)
    below = lax.ppermute(block[:, 0], axes, up)
    return above, below


def row_beside(edges):
    axes = ("y", "z", "x")
    count = lax.axis_size(("z", "x"))
    pairs = []
    for y in range(LINE):
        for i in range(count):
            j = i + 1 if y % 2 == 0 else i - 1
            if 0 <= j < count:
                pairs.append((y * count + i, y * count + j))
    return lax.ppermute(edges, axes, pairs)


def along_line(blocks):
    return lax.all_to_all(blocks, "y", 0, 0, tiled=True, axis_index_groups=[list(ORDER)])


def call(kernel, shape, inputs, scratch=(), kind=BF16, limit=16):
    spaces = [pltpu.HBM if far else pltpu.VMEM for _, far in inputs]
    return pl.pallas_call(
        kernel,
        out_shape=jax.ShapeDtypeStruct(shape, kind),
        in_specs=[pl.BlockSpec(memory_space=space) for space in spaces],
        out_specs=pl.BlockSpec(memory_space=pltpu.VMEM),
        scratch_shapes=list(scratch),
        compiler_params=pltpu.CompilerParams(vmem_limit_bytes=limit * 1024 * 1024),
    )(*[array for array, _ in inputs])


def local(latent, gain_first, conv_first, bias_first, conv_upper, bias_upper):
    other = lax.ppermute(conv_first, "y", [(i, i ^ 1) for i in range(LINE)])
    acts = call(
        act_kernel,
        (LINE, 2 * PART, SENT),
        [(latent, True), (gain_first, True)],
        [
            pltpu.VMEM(latent.shape, BF16),
            pltpu.VMEM(gain_first.shape, F32),
            pltpu.SemaphoreType.DMA((2,)),
        ],
        limit=60,
    )
    acts, conv_first, conv_upper = lax.optimization_barrier((acts, conv_first, conv_upper))
    own = lax.all_gather(conv_first, "core", axis=1, tiled=True)
    other = lax.all_gather(other, "core", axis=1, tiled=True)
    upper = jnp.swapaxes(conv_upper, 1, 2)
    upper = jnp.concatenate([upper, upper], axis=1)
    acts = along_line(acts)
    acts, own, other = lax.optimization_barrier((acts, own, other))
    acts = lax.all_gather(acts, "core", axis=0, tiled=False)
    edges = row_beside(call(pack_kernel, (2, 2, 2 * PART, SENT), [(acts, False)]))
    parts = call(
        inner_kernel,
        (LINE, FRAMES, HALF, COLS, CHANS),
        [(acts, False), (own, True), (other, True)],
        [
            pltpu.VMEM((PAIRS, 2 * PART, 2 * SENT), BF16),
            pltpu.VMEM((PAIRS, 2 * PART, 2 * SENT), BF16),
            pltpu.VMEM((2, 27 * PART, LINE * CELLS), BF16),
            pltpu.VMEM((2, 27, PART, CHANS), BF16),
            pltpu.SemaphoreType.DMA((2,)),
        ],
        kind=F32,
        limit=32,
    )
    parts = call(
        edge_kernel,
        (LINE, CELLS, CHANS),
        [(edges, False), (parts, False), (own, True), (other, True)],
        [
            pltpu.VMEM((2, 9 * PART, EDGE), BF16),
            pltpu.VMEM((2, 3, 3, PART, CHANS), BF16),
            pltpu.SemaphoreType.DMA((2, 3)),
        ],
    )
    parts = along_line(parts)
    block = call(
        block_kernel,
        (FRAMES, ROWS, COLS, CHANS),
        [(parts, False), (latent, False), (bias_first, False), (upper, True)],
    )
    above, below = row_neighbours(block)
    inner = call(
        upper_inner_kernel,
        (COLS, FRAMES * 2 * ROWS, 6 * OUTS),
        [(block, False), (upper, False)],
        kind=F32,
    )
    out = call(
        upper_kernel,
        (FRAMES * 2 * ROWS, 2 * COLS * OUTS),
        [(array, False) for array in (above, below, inner, upper, bias_upper)],
    )
    return out.reshape(FRAMES, 2 * ROWS, 2 * COLS * OUTS)


def solution(mesh):
    fine = Mesh(mesh.devices.reshape(8, 2, 8, 4), ("y", "core", "z", "x"))
    tm, rows = ("y", "core"), ("z", "x")
    in_specs = (P(tm, rows, None, None), P(), P(None, tm, None), P(), P(), P())
    return jax.shard_map(
        local, mesh=fine, in_specs=in_specs, out_specs=P(tm, rows, None), check_vma=False
    )
```

```python
import jax
import jax.numpy as jnp
from jax import lax
from jax.experimental import pallas as pl
from jax.experimental.pallas import tpu as pltpu
from jax.sharding import Mesh
from jax.sharding import PartitionSpec as P

F32 = jnp.float32
BF16 = jnp.bfloat16
FRAMES, ROWS, COLS, CHANS, OUTS = 2, 4, 16, 384, 192
LINE = 8
PART = CHANS // LINE
PAIRS = LINE // 2
HALF = ROWS // 2
CELLS = FRAMES * HALF * COLS
SENT = FRAMES * ROWS * COLS
EDGE = LINE * FRAMES * COLS
ORDER = (4, 5, 6, 7, 0, 1, 2, 3)
SLOT = tuple(ORDER.index(y) for y in range(LINE))
NT_DIMS = (((1,), (1,)), ((), ()))
TN_DIMS = (((0,), (0,)), ((), ()))


def one_hot(wanted, there):
    return jnp.where(wanted == there, 1.0, 0.0).astype(BF16)


def window_picks(half):
    lane = lax.broadcasted_iota(jnp.int32, (1, 18 * CELLS), 1)
    tap, frame, row, col = lane >> 7, (lane >> 5) & 3, ((lane >> 4) & 1) ^ half, lane & 15
    dy = (tap * 11) >> 5
    col = col + tap - 3 * dy - 1
    row = row + dy - 1 + 2 * half
    wanted = (frame << 6) + (row << 4) + col
    inside = (col >= 0) & (col < COLS) & (row >= 0) & (row < ROWS)
    wanted = jnp.where(inside, wanted, -1)
    return one_hot(wanted, lax.broadcasted_iota(jnp.int32, (2 * SENT, 18 * CELLS), 0))


def edge_picks():
    lane = lax.broadcasted_iota(jnp.int32, (1, 3 * EDGE), 1)
    col = (lane & 15) + (lane >> 8) - 1
    wanted = (((lane >> 4) & 15) << 4) + col
    wanted = jnp.where((col >= 0) & (col < COLS), wanted, -1)
    return one_hot(wanted, lax.broadcasted_iota(jnp.int32, (EDGE, 3 * EDGE), 0))


def row_picks():
    shape = (6 * ROWS * COLS * FRAMES, SENT)
    place = lax.broadcasted_iota(jnp.int32, (shape[0], 1), 0)
    dy, col, frame, i = place >> 8, (place >> 4) & 15, (place >> 3) & 1, place & 7
    row = ((i + dy + 1) >> 1) - 1
    wanted = (frame << 6) + (row << 4) + col
    wanted = jnp.where((row >= 0) & (row < ROWS), wanted, -1)
    return one_hot(wanted, lax.broadcasted_iota(jnp.int32, shape, 1))


def scaled_silu(block, gain):
    values = block.astype(F32)
    mean_square = jnp.mean(values * values, axis=-1, keepdims=True)
    scaled = values * lax.rsqrt(mean_square + 1e-06) * gain
    return (scaled / (1.0 + jnp.exp(-scaled))).astype(BF16)


def act_kernel(lat_ref, gain_ref, out_ref, lat, gain, arrived):
    copies = [
        pltpu.make_async_copy(lat_ref, lat, arrived.at[0]),
        pltpu.make_async_copy(gain_ref, gain, arrived.at[1]),
    ]
    for copy in copies:
        copy.start()
    row = lax.broadcasted_iota(jnp.int32, (CHANS, CHANS), 0)
    col = lax.broadcasted_iota(jnp.int32, (CHANS, CHANS), 1)
    eye = one_hot(row, col)
    for copy in copies:
        copy.wait()
    act = scaled_silu(lat[...].reshape(SENT, CHANS), gain[...].reshape(1, CHANS))
    flipped = lax.dot_general(eye, act, NT_DIMS, preferred_element_type=F32).astype(BF16)
    for y in range(LINE):
        start = (y // 2) * 2 * PART
        out_ref[SLOT[y]] = flipped[start : start + 2 * PART]


def places():
    mine = lax.axis_index("y") & 1
    return lax.axis_index("core"), mine, mine ^ (lax.axis_index("x") & 1)


def pack_kernel(act_ref, out_ref):
    _, _, half = places()
    row = (ROWS - 1) * half
    lane = lax.broadcasted_iota(jnp.int32, (1, SENT), 1)
    wanted = ((lane >> 4) << 6) + (row << 4) + (lane & 15)
    picks = one_hot(wanted, lax.broadcasted_iota(jnp.int32, (4 * SENT, SENT), 0))
    for core in range(2):
        for group in range(2):
            block = jnp.concatenate([act_ref[core, SLOT[4 * group + k]] for k in range(4)], axis=1)
            packed = jnp.dot(block, picks, preferred_element_type=F32)
            out_ref[core, group] = packed.astype(BF16)


def weight_dots(blocks, weights, mine):
    total = None
    for i in range(2):
        rows = blocks.shape[1]
        part = lax.dot_general(
            blocks[mine if i == 0 else 1 - mine],
            weights[i].reshape(rows, CHANS),
            TN_DIMS,
            preferred_element_type=F32,
        )
        total = part if total is None else total + part
    return total


def inner_kernel(
    act_ref,
    own_ref,
    other_ref,
    out_ref,
    taps_ref,
    here,
    before,
    windows,
    weights,
    arrived,
):
    core, mine, half = places()
    copies = [
        pltpu.make_async_copy(ref, weights.at[i], arrived.at[i])
        for i, ref in enumerate((own_ref, other_ref))
    ]
    for copy in copies:
        copy.start()
    for y in range(LINE):
        where = (y // 2, slice(None), slice((y % 2) * SENT, (y % 2 + 1) * SENT))
        here[where] = act_ref[core, SLOT[y]]

        @pl.when(core == 1)
        def _():
            before[where] = act_ref[0, SLOT[y]]

        @pl.when(core == 0)
        def _():
            before[where] = act_ref[1, SLOT[y - 1]] if y else jnp.zeros_like(act_ref[1, 0])

    now = here[...].reshape(PAIRS * 2 * PART, 2 * SENT)
    prior = before[...].reshape(PAIRS * 2 * PART, 2 * SENT)
    picks = window_picks(half)
    earliest = jnp.dot(prior, picks, preferred_element_type=F32)
    latest = jnp.dot(now, picks, preferred_element_type=F32)
    lanes = 2 * CELLS
    step = lanes // 4
    frame = (lax.broadcasted_iota(jnp.int32, (PAIRS * 2 * PART, lanes), 1) >> 5) & 1
    for tap in range(9):
        first = earliest[:, tap * lanes : (tap + 1) * lanes]
        last = latest[:, tap * lanes : (tap + 1) * lanes]
        middle = jnp.where(
            frame == 0, pltpu.roll(first, lanes - step, 1), pltpu.roll(last, step, 1)
        )
        for dt, taken in enumerate((first, middle, last)):
            taken = taken.astype(BF16)
            for pair in range(PAIRS):
                for part in range(2):
                    row = (2 * pair + part) * PART
                    windows[
                        part,
                        (9 * dt + tap) * PART : (9 * dt + tap + 1) * PART,
                        pair * lanes : (pair + 1) * lanes,
                    ] = taken[row : row + PART]
    for copy in copies:
        copy.wait()
    for i in range(2):
        for dt in range(3):
            taps_ref[i, dt] = weights[i, pl.ds(9 * dt + 6 * half, 3)]
    sums = weight_dots(windows, weights, mine)
    out_ref[...] = sums.reshape(out_ref.shape)


def edge_kernel(edge_ref, part_ref, taps_ref, out_ref, windows):
    core, mine, half = places()

    def line_of(which):
        return jnp.concatenate([edge_ref[which, 0], edge_ref[which, 1]], axis=1)

    chip = 2 * COLS
    prior = line_of(1 - core).astype(F32)
    lane = lax.broadcasted_iota(jnp.int32, prior.shape, 1)
    later = jnp.where(lane < chip, 0.0, pltpu.roll(prior, chip, 1))
    prior = jnp.where(core == 0, later, prior).astype(BF16)
    both = jnp.concatenate([prior, line_of(core)], axis=0)
    taken = jnp.dot(both, edge_picks(), preferred_element_type=F32)
    frame = (lax.broadcasted_iota(jnp.int32, (2 * PART, EDGE), 1) >> 4) & 1
    for dx in range(3):
        first = taken[: 2 * PART, dx * EDGE : (dx + 1) * EDGE]
        last = taken[2 * PART :, dx * EDGE : (dx + 1) * EDGE]
        middle = jnp.where(
            frame == 0, pltpu.roll(first, EDGE - COLS, 1), pltpu.roll(last, COLS, 1)
        )
        for dt, window in enumerate((first, middle, last)):
            window = window.astype(BF16)
            for part in range(2):
                row = (3 * dt + dx) * PART
                windows[part, row : row + PART] = window[part * PART : (part + 1) * PART]
    sums = weight_dots(windows, taps_ref, mine)
    for y in range(LINE):
        for f in range(FRAMES):
            start = (2 * y + f) * COLS
            border = part_ref[y, f, 0] + sums[start : start + COLS]
            row = f * HALF * COLS
            out_ref[SLOT[y], row : row + COLS] = border.astype(BF16)
            out_ref[SLOT[y], row + COLS : row + 2 * COLS] = part_ref[y, f, 1].astype(BF16)


def block_kernel(part_ref, lat_ref, bias_ref, later_ref, out_ref, far_ref, near_ref):
    del later_ref
    bias = bias_ref[...].reshape(1, CHANS)
    odd = lax.axis_index("x") & 1
    for mine in range(2):
        total = part_ref[SLOT[mine]].astype(F32)
        for y in range(mine + 2, LINE, 2):
            total = total + part_ref[SLOT[y]].astype(F32)
        total = total + bias
        half = mine ^ odd
        for f in range(FRAMES):
            for inside in range(HALF):
                row = half * HALF + (inside ^ half)
                start = (f * HALF + inside) * COLS
                value = lat_ref[f, row].astype(F32) + total[start : start + COLS]
                out_ref[f, row] = value.astype(BF16)

    @pl.when(odd == 1)
    def _():
        far_ref[...] = out_ref[:, ROWS - 1]
        near_ref[...] = out_ref[:, 0]

    @pl.when(odd == 0)
    def _():
        far_ref[...] = out_ref[:, 0]
        near_ref[...] = out_ref[:, ROWS - 1]


def upper_inner_kernel(block_ref, weight_ref, out_ref):
    rows = jnp.dot(
        row_picks(), block_ref[...].reshape(SENT, CHANS), preferred_element_type=F32
    ).astype(BF16)
    cells = COLS * FRAMES * 2 * ROWS
    total = None
    for dy in range(3):
        part = lax.dot_general(
            rows[dy * cells : (dy + 1) * cells],
            weight_ref[3 * dy : 3 * dy + 3].reshape(6 * OUTS, CHANS),
            NT_DIMS,
            preferred_element_type=F32,
        )
        total = part if total is None else total + part
    out_ref[...] = total.reshape(out_ref.shape)


def upper_kernel(far_ref, near_ref, inner_ref, weight_ref, bias_ref, out_ref):
    wide = 2 * OUTS
    lines = FRAMES * 2 * ROWS

    far = far_ref[...].reshape(FRAMES * COLS, CHANS).astype(F32)
    near = near_ref[...].reshape(FRAMES * COLS, CHANS).astype(F32)
    odd = lax.axis_index("x") & 1

    def taps(row, dy):
        return lax.dot_general(
            row.astype(BF16),
            weight_ref[3 * dy : 3 * dy + 3].reshape(3 * wide, CHANS),
            NT_DIMS,
            preferred_element_type=F32,
        )

    above = taps(jnp.where(odd == 1, near, far), 0)
    below = taps(jnp.where(odd == 1, far, near), 2)
    line = lax.broadcasted_iota(jnp.int32, (lines, 3 * wide), 0)
    totals = []
    for c in range(COLS):
        total = inner_ref[c]
        for f in range(FRAMES):
            row = f * COLS + c
            top, bottom = f * 2 * ROWS, (f + 1) * 2 * ROWS - 1
            total = total + jnp.where(line == top, above[row : row + 1], 0.0)
            total = total + jnp.where(line == bottom, below[row : row + 1], 0.0)
        totals.append(total)
    bias = bias_ref[...].reshape(1, OUTS)
    bias = jnp.concatenate([bias, bias], axis=1)
    left = lax.broadcasted_iota(jnp.int32, (lines, wide), 1) < OUTS
    zero = jnp.zeros((lines, wide), F32)
    for c in range(COLS):
        first_before = totals[c - 1][:, :wide] if c else zero
        last_after = totals[c + 1][:, 2 * wide :] if c < COLS - 1 else zero
        value = (
            jnp.where(left, first_before, totals[c][:, :wide])
            + totals[c][:, wide : 2 * wide]
            + jnp.where(left, totals[c][:, 2 * wide :], last_after)
            + bias
        )
        out_ref[:, c * wide : (c + 1) * wide] = value.astype(BF16)


def swapped(row, first):
    axes = ("z", "x")
    pairs = []
    for i in range(first, lax.axis_size(axes) - 1, 2):
        pairs += [(i, i + 1), (i + 1, i)]
    return lax.ppermute(row, axes, pairs)


def row_beside(edges):
    count = lax.axis_size(("z", "x"))
    pairs = []
    for y in range(LINE):
        for i in range(1 - y % 2, count - 1, 2):
            here, there = y * count + i, y * count + i + 1
            pairs += [(here, there), (there, here)]
    return lax.ppermute(edges, ("y", "z", "x"), pairs)


def along_line(blocks):
    return lax.all_to_all(blocks, "y", 0, 0, tiled=True, axis_index_groups=[list(ORDER)])


def call(kernel, outs, inputs, scratch=(), limit=16):
    spaces = [pltpu.HBM if far else pltpu.VMEM for _, far in inputs]
    return pl.pallas_call(
        kernel,
        out_shape=[jax.ShapeDtypeStruct(shape, kind) for shape, kind in outs],
        in_specs=[pl.BlockSpec(memory_space=space) for space in spaces],
        out_specs=[pl.BlockSpec(memory_space=pltpu.VMEM) for _ in outs],
        scratch_shapes=list(scratch),
        compiler_params=pltpu.CompilerParams(vmem_limit_bytes=limit * 1024 * 1024),
    )(*[array for array, _ in inputs])


def local(latent, gain_first, conv_first, bias_first, conv_upper, bias_upper):
    other = lax.ppermute(conv_first, "y", [(i, i ^ 1) for i in range(LINE)])
    (acts,) = call(
        act_kernel,
        [((LINE, 2 * PART, SENT), BF16)],
        [(latent, True), (gain_first, True)],
        [
            pltpu.VMEM(latent.shape, BF16),
            pltpu.VMEM(gain_first.shape, F32),
            pltpu.SemaphoreType.DMA((2,)),
        ],
        limit=60,
    )
    acts, conv_first, conv_upper = lax.optimization_barrier((acts, conv_first, conv_upper))
    own = lax.all_gather(conv_first, "core", axis=1, tiled=True)
    other = lax.all_gather(other, "core", axis=1, tiled=True)
    upper = jnp.swapaxes(conv_upper, 1, 2)
    upper = jnp.concatenate([upper, upper], axis=1)
    acts = along_line(acts)
    acts, own, other = lax.optimization_barrier((acts, own, other))
    acts = lax.all_gather(acts, "core", axis=0, tiled=False)
    (edges,) = call(pack_kernel, [((2, 2, 2 * PART, SENT), BF16)], [(acts, False)])
    edges = row_beside(edges)
    parts, taps = call(
        inner_kernel,
        [((LINE, FRAMES, HALF, COLS, CHANS), F32), ((2, 3, 3, PART, CHANS), BF16)],
        [(acts, False), (own, True), (other, True)],
        [
            pltpu.VMEM((PAIRS, 2 * PART, 2 * SENT), BF16),
            pltpu.VMEM((PAIRS, 2 * PART, 2 * SENT), BF16),
            pltpu.VMEM((2, 27 * PART, LINE * CELLS), BF16),
            pltpu.VMEM((2, 27, PART, CHANS), BF16),
            pltpu.SemaphoreType.DMA((2,)),
        ],
        limit=32,
    )
    (parts,) = call(
        edge_kernel,
        [((LINE, CELLS, CHANS), BF16)],
        [(edges, False), (parts, False), (taps, False)],
        [pltpu.VMEM((2, 9 * PART, EDGE), BF16)],
    )
    parts = along_line(parts)
    row = ((FRAMES, COLS, CHANS), BF16)
    block, far, near = call(
        block_kernel,
        [((FRAMES, ROWS, COLS, CHANS), BF16), row, row],
        [(parts, False), (latent, False), (bias_first, False), (upper, True)],
    )
    far, near = swapped(far, 1), swapped(near, 0)
    (inner,) = call(
        upper_inner_kernel,
        [((COLS, FRAMES * 2 * ROWS, 6 * OUTS), F32)],
        [(block, False), (upper, False)],
    )
    (out,) = call(
        upper_kernel,
        [((FRAMES * 2 * ROWS, 2 * COLS * OUTS), BF16)],
        [(array, False) for array in (far, near, inner, upper, bias_upper)],
    )
    return out.reshape(FRAMES, 2 * ROWS, 2 * COLS * OUTS)


def solution(mesh):
    fine = Mesh(mesh.devices.reshape(8, 2, 8, 4), ("y", "core", "z", "x"))
    tm, rows = ("y", "core"), ("z", "x")
    in_specs = (P(tm, rows, None, None), P(), P(None, tm, None), P(), P(), P())
    return jax.shard_map(
        local, mesh=fine, in_specs=in_specs, out_specs=P(tm, rows, None), check_vma=False
    )
```

```python
import jax
import jax.numpy as jnp
from jax import lax
from jax.experimental import pallas as pl
from jax.experimental.pallas import tpu as pltpu
from jax.sharding import Mesh
from jax.sharding import PartitionSpec as P

F32 = jnp.float32
BF16 = jnp.bfloat16
FRAMES, ROWS, COLS, CHANS, OUTS = 2, 4, 16, 384, 192
LINE = 8
PART = CHANS // LINE
PAIRS = LINE // 2
HALF = ROWS // 2
CELLS = FRAMES * HALF * COLS
SENT = FRAMES * ROWS * COLS
ORDER = (4, 5, 6, 7, 0, 1, 2, 3)
SLOT = tuple(ORDER.index(y) for y in range(LINE))
NT_DIMS = (((1,), (1,)), ((), ()))
TN_DIMS = (((0,), (0,)), ((), ()))


def one_hot(wanted, there):
    return jnp.where(wanted == there, 1.0, 0.0).astype(BF16)


def window_picks():
    lane = lax.broadcasted_iota(jnp.int32, (1, 18 * CELLS), 1)
    tap, frame, row, col = lane >> 7, (lane >> 5) & 3, (lane >> 4) & 1, lane & 15
    dy = (tap * 11) >> 5
    col = col + tap - 3 * dy - 1
    wanted = (frame << 6) + ((row + dy) << 4) + col
    wanted = jnp.where((col >= 0) & (col < COLS), wanted, -1)
    return one_hot(wanted, lax.broadcasted_iota(jnp.int32, (2 * SENT, 18 * CELLS), 0))


def row_picks():
    shape = (6 * ROWS * COLS * FRAMES, SENT)
    place = lax.broadcasted_iota(jnp.int32, (shape[0], 1), 0)
    dy, col, frame, i = place >> 8, (place >> 4) & 15, (place >> 3) & 1, place & 7
    row = ((i + dy + 1) >> 1) - 1
    wanted = (frame << 6) + (row << 4) + col
    wanted = jnp.where((row >= 0) & (row < ROWS), wanted, -1)
    return one_hot(wanted, lax.broadcasted_iota(jnp.int32, shape, 1))


def scaled_silu(block, gain):
    values = block.astype(F32)
    mean_square = jnp.mean(values * values, axis=-1, keepdims=True)
    scaled = values * lax.rsqrt(mean_square + 1e-06) * gain
    return scaled / (1.0 + jnp.exp(-scaled))


def own_kernel(lat_ref, gain_ref, out_ref):
    out_ref[...] = scaled_silu(
        lat_ref[...].reshape(SENT, CHANS), gain_ref[...].reshape(1, CHANS)
    )


def act_kernel(far_ref, near_ref, own_ref, gain_ref, out_ref):
    odd = lax.axis_index("x") & 1
    count = FRAMES * COLS
    far = far_ref[...].reshape(count, CHANS).astype(F32)
    near = near_ref[...].reshape(count, CHANS).astype(F32)
    edges = jnp.concatenate(
        [jnp.where(odd == 1, near, far), jnp.where(odd == 1, far, near)], axis=0
    )
    edges = scaled_silu(edges, gain_ref[...].reshape(1, CHANS))
    own = own_ref[...]
    size = (HALF + 1) * COLS
    for half in range(2):
        cells = []
        for f in range(FRAMES):
            start = (f * ROWS + half * (HALF - 1)) * COLS
            beside = (half * FRAMES + f) * COLS
            parts = [edges[beside : beside + COLS], own[start : start + size]]
            cells += parts if half == 0 else parts[::-1]
        flipped = jnp.concatenate(cells, axis=0).T.astype(BF16)
        for pair in range(PAIRS):
            start = pair * 2 * PART
            out_ref[SLOT[2 * pair + half]] = flipped[start : start + 2 * PART]


def weight_dots(blocks, weights, mine):
    total = None
    for i in range(2):
        rows = blocks.shape[1]
        part = lax.dot_general(
            blocks[mine if i == 0 else 1 - mine],
            weights[i][...].reshape(rows, CHANS),
            TN_DIMS,
            preferred_element_type=F32,
        )
        total = part if total is None else total + part
    return total


def inner_kernel(act_ref, own_ref, other_ref, out_ref, here, before, windows):
    core, mine = lax.axis_index("core"), lax.axis_index("y") & 1
    for y in range(LINE):
        where = (y // 2, slice(None), slice((y % 2) * SENT, (y % 2 + 1) * SENT))
        here[where] = act_ref[core, SLOT[y]]

        @pl.when(core == 1)
        def _():
            before[where] = act_ref[0, SLOT[y]]

        @pl.when(core == 0)
        def _():
            before[where] = act_ref[1, SLOT[y - 1]] if y else jnp.zeros_like(act_ref[1, 0])

    now = here[...].reshape(PAIRS * 2 * PART, 2 * SENT)
    prior = before[...].reshape(PAIRS * 2 * PART, 2 * SENT)
    picks = window_picks()
    earliest = jnp.dot(prior, picks, preferred_element_type=F32)
    latest = jnp.dot(now, picks, preferred_element_type=F32)
    lanes = 2 * CELLS
    step = lanes // 4
    frame = (lax.broadcasted_iota(jnp.int32, (PAIRS * 2 * PART, lanes), 1) >> 5) & 1
    for tap in range(9):
        first = earliest[:, tap * lanes : (tap + 1) * lanes]
        last = latest[:, tap * lanes : (tap + 1) * lanes]
        middle = jnp.where(
            frame == 0, pltpu.roll(first, lanes - step, 1), pltpu.roll(last, step, 1)
        )
        for dt, taken in enumerate((first, middle, last)):
            taken = taken.astype(BF16)
            for pair in range(PAIRS):
                for part in range(2):
                    row = (2 * pair + part) * PART
                    windows[
                        part,
                        (9 * dt + tap) * PART : (9 * dt + tap + 1) * PART,
                        pair * lanes : (pair + 1) * lanes,
                    ] = taken[row : row + PART]
    sums = weight_dots(windows, (own_ref, other_ref), mine).astype(BF16)
    for y in range(LINE):
        out_ref[SLOT[y]] = sums[y * CELLS : (y + 1) * CELLS]


def block_kernel(part_ref, lat_ref, bias_ref, later_ref, out_ref, far_ref, near_ref):
    del later_ref
    bias = bias_ref[...].reshape(1, CHANS)
    odd = lax.axis_index("x") & 1
    for half in range(2):
        total = part_ref[SLOT[half]].astype(F32)
        for y in range(half + 2, LINE, 2):
            total = total + part_ref[SLOT[y]].astype(F32)
        total = total + bias
        for f in range(FRAMES):
            for inside in range(HALF):
                row = half * HALF + inside
                start = (f * HALF + inside) * COLS
                value = lat_ref[f, row].astype(F32) + total[start : start + COLS]
                out_ref[f, row] = value.astype(BF16)

    @pl.when(odd == 1)
    def _():
        far_ref[...] = out_ref[:, ROWS - 1]
        near_ref[...] = out_ref[:, 0]

    @pl.when(odd == 0)
    def _():
        far_ref[...] = out_ref[:, 0]
        near_ref[...] = out_ref[:, ROWS - 1]


def upper_inner_kernel(block_ref, weight_ref, out_ref):
    rows = jnp.dot(
        row_picks(), block_ref[...].reshape(SENT, CHANS), preferred_element_type=F32
    ).astype(BF16)
    cells = COLS * FRAMES * 2 * ROWS
    total = None
    for dy in range(3):
        part = lax.dot_general(
            rows[dy * cells : (dy + 1) * cells],
            weight_ref[3 * dy : 3 * dy + 3].reshape(6 * OUTS, CHANS),
            NT_DIMS,
            preferred_element_type=F32,
        )
        total = part if total is None else total + part
    out_ref[...] = total.reshape(out_ref.shape)


def upper_kernel(far_ref, near_ref, inner_ref, weight_ref, bias_ref, out_ref):
    wide = 2 * OUTS
    lines = FRAMES * 2 * ROWS

    far = far_ref[...].reshape(FRAMES * COLS, CHANS).astype(F32)
    near = near_ref[...].reshape(FRAMES * COLS, CHANS).astype(F32)
    odd = lax.axis_index("x") & 1

    def taps(row, dy):
        return lax.dot_general(
            row.astype(BF16),
            weight_ref[3 * dy : 3 * dy + 3].reshape(3 * wide, CHANS),
            NT_DIMS,
            preferred_element_type=F32,
        )

    above = taps(jnp.where(odd == 1, near, far), 0)
    below = taps(jnp.where(odd == 1, far, near), 2)
    line = lax.broadcasted_iota(jnp.int32, (lines, 3 * wide), 0)
    totals = []
    for c in range(COLS):
        total = inner_ref[c]
        for f in range(FRAMES):
            row = f * COLS + c
            top, bottom = f * 2 * ROWS, (f + 1) * 2 * ROWS - 1
            total = total + jnp.where(line == top, above[row : row + 1], 0.0)
            total = total + jnp.where(line == bottom, below[row : row + 1], 0.0)
        totals.append(total)
    bias = bias_ref[...].reshape(1, OUTS)
    bias = jnp.concatenate([bias, bias], axis=1)
    left = lax.broadcasted_iota(jnp.int32, (lines, wide), 1) < OUTS
    zero = jnp.zeros((lines, wide), F32)
    for c in range(COLS):
        first_before = totals[c - 1][:, :wide] if c else zero
        last_after = totals[c + 1][:, 2 * wide :] if c < COLS - 1 else zero
        value = (
            jnp.where(left, first_before, totals[c][:, :wide])
            + totals[c][:, wide : 2 * wide]
            + jnp.where(left, totals[c][:, 2 * wide :], last_after)
            + bias
        )
        out_ref[:, c * wide : (c + 1) * wide] = value.astype(BF16)


def swapped(row, first):
    axes = ("z", "x")
    pairs = []
    for i in range(first, lax.axis_size(axes) - 1, 2):
        pairs += [(i, i + 1), (i + 1, i)]
    return lax.ppermute(row, axes, pairs)


def along_line(blocks):
    return lax.all_to_all(blocks, "y", 0, 0, tiled=True, axis_index_groups=[list(ORDER)])


def call(kernel, outs, inputs, scratch=(), limit=16):
    spaces = [pltpu.HBM if far else pltpu.VMEM for _, far in inputs]
    return pl.pallas_call(
        kernel,
        out_shape=[jax.ShapeDtypeStruct(shape, kind) for shape, kind in outs],
        in_specs=[pl.BlockSpec(memory_space=space) for space in spaces],
        out_specs=[pl.BlockSpec(memory_space=pltpu.VMEM) for _ in outs],
        scratch_shapes=list(scratch),
        compiler_params=pltpu.CompilerParams(vmem_limit_bytes=limit * 1024 * 1024),
    )(*[array for array, _ in inputs])


def local(latent, gain_first, conv_first, bias_first, conv_upper, bias_upper):
    odd = (lax.axis_index("x") & 1) == 1
    first, last = latent[:, 0], latent[:, ROWS - 1]
    far, near = jnp.where(odd, last, first), jnp.where(odd, first, last)
    far, near, conv_first = lax.optimization_barrier((far, near, conv_first))
    far, near = swapped(far, 1), swapped(near, 0)
    other = lax.ppermute(conv_first, "y", [(i, i ^ 1) for i in range(LINE)])
    (own_acts,) = call(
        own_kernel, [((SENT, CHANS), F32)], [(latent, False), (gain_first, False)]
    )
    (acts,) = call(
        act_kernel,
        [((LINE, 2 * PART, SENT), BF16)],
        [(array, False) for array in (far, near, own_acts, gain_first)],
    )
    acts, conv_first, conv_upper = lax.optimization_barrier((acts, conv_first, conv_upper))
    own = lax.all_gather(conv_first, "core", axis=1, tiled=True)
    other = lax.all_gather(other, "core", axis=1, tiled=True)
    upper = jnp.swapaxes(conv_upper, 1, 2)
    upper = jnp.concatenate([upper, upper], axis=1)
    acts = along_line(acts)
    acts, own, other = lax.optimization_barrier((acts, own, other))
    acts = lax.all_gather(acts, "core", axis=0, tiled=False)
    (parts,) = call(
        inner_kernel,
        [((LINE, CELLS, CHANS), BF16)],
        [(acts, False), (own, False), (other, False)],
        [
            pltpu.VMEM((PAIRS, 2 * PART, 2 * SENT), BF16),
            pltpu.VMEM((PAIRS, 2 * PART, 2 * SENT), BF16),
            pltpu.VMEM((2, 27 * PART, LINE * CELLS), BF16),
        ],
        limit=24,
    )
    parts = along_line(parts)
    row = ((FRAMES, COLS, CHANS), BF16)
    block, far, near = call(
        block_kernel,
        [((FRAMES, ROWS, COLS, CHANS), BF16), row, row],
        [(parts, False), (latent, False), (bias_first, False), (upper, True)],
    )
    far, near = swapped(far, 1), swapped(near, 0)
    (inner,) = call(
        upper_inner_kernel,
        [((COLS, FRAMES * 2 * ROWS, 6 * OUTS), F32)],
        [(block, False), (upper, False)],
    )
    (out,) = call(
        upper_kernel,
        [((FRAMES * 2 * ROWS, 2 * COLS * OUTS), BF16)],
        [(array, False) for array in (far, near, inner, upper, bias_upper)],
    )
    return out.reshape(FRAMES, 2 * ROWS, 2 * COLS * OUTS)


def solution(mesh):
    fine = Mesh(mesh.devices.reshape(8, 2, 8, 4), ("y", "core", "z", "x"))
    tm, rows = ("y", "core"), ("z", "x")
    in_specs = (P(tm, rows, None, None), P(), P(None, tm, None), P(), P(), P())
    return jax.shard_map(
        local, mesh=fine, in_specs=in_specs, out_specs=P(tm, rows, None), check_vma=False
    )
```

```python
import jax
import jax.numpy as jnp
from jax import lax
from jax.experimental import pallas as pl
from jax.experimental.pallas import tpu as pltpu
from jax.sharding import Mesh
from jax.sharding import PartitionSpec as P

F32 = jnp.float32
BF16 = jnp.bfloat16
FRAMES, ROWS, COLS, CHANS, OUTS = 2, 4, 16, 384, 192
LINE = 8
PART = CHANS // LINE
PAIRS = LINE // 2
HALF = ROWS // 2
CELLS = FRAMES * HALF * COLS
SENT = FRAMES * ROWS * COLS
ORDER = (4, 6, 0, 2, 5, 7, 1, 3)
SLOT = tuple(ORDER.index(y) for y in range(LINE))
NT_DIMS = (((1,), (1,)), ((), ()))
TN_DIMS = (((0,), (0,)), ((), ()))


def one_hot(wanted, there):
    return jnp.where(wanted == there, 1.0, 0.0).astype(BF16)


def window_picks():
    lane = lax.broadcasted_iota(jnp.int32, (1, 18 * CELLS), 1)
    tap, frame, row, col = lane >> 7, (lane >> 5) & 3, (lane >> 4) & 1, lane & 15
    dy = (tap * 11) >> 5
    col = col + tap - 3 * dy - 1
    wanted = (frame << 6) + ((row + dy) << 4) + col
    wanted = jnp.where((col >= 0) & (col < COLS), wanted, -1)
    return one_hot(wanted, lax.broadcasted_iota(jnp.int32, (2 * SENT, 18 * CELLS), 0))


def row_picks():
    shape = (6 * ROWS * COLS * FRAMES, SENT)
    place = lax.broadcasted_iota(jnp.int32, (shape[0], 1), 0)
    dy, col, frame, i = place >> 8, (place >> 4) & 15, (place >> 3) & 1, place & 7
    row = ((i + dy + 1) >> 1) - 1
    wanted = (frame << 6) + (row << 4) + col
    wanted = jnp.where((row >= 0) & (row < ROWS), wanted, -1)
    return one_hot(wanted, lax.broadcasted_iota(jnp.int32, shape, 1))


def scaled_silu(block, gain):
    values = block.astype(F32)
    mean_square = jnp.mean(values * values, axis=-1, keepdims=True)
    scaled = values * lax.rsqrt(mean_square + 1e-06) * gain
    return scaled / (1.0 + jnp.exp(-scaled))


def own_kernel(lat_ref, gain_ref, out_ref):
    out_ref[...] = scaled_silu(
        lat_ref[...].reshape(SENT, CHANS), gain_ref[...].reshape(1, CHANS)
    )


def act_kernel(far_ref, near_ref, own_ref, gain_ref, out_ref):
    odd = lax.axis_index("x") & 1
    count = FRAMES * COLS
    far = far_ref[...].reshape(count, CHANS).astype(F32)
    near = near_ref[...].reshape(count, CHANS).astype(F32)
    edges = jnp.concatenate(
        [jnp.where(odd == 1, near, far), jnp.where(odd == 1, far, near)], axis=0
    )
    edges = scaled_silu(edges, gain_ref[...].reshape(1, CHANS))
    own = own_ref[...]
    size = (HALF + 1) * COLS
    for half in range(2):
        cells = []
        for f in range(FRAMES):
            start = (f * ROWS + half * (HALF - 1)) * COLS
            beside = (half * FRAMES + f) * COLS
            parts = [edges[beside : beside + COLS], own[start : start + size]]
            cells += parts if half == 0 else parts[::-1]
        flipped = jnp.concatenate(cells, axis=0).T.astype(BF16)
        for pair in range(PAIRS):
            start = pair * 2 * PART
            out_ref[SLOT[2 * pair + half]] = flipped[start : start + 2 * PART]


def weight_dots(blocks, weights, mine):
    total = None
    for i in range(2):
        rows = blocks.shape[1]
        part = lax.dot_general(
            blocks[mine if i == 0 else 1 - mine],
            weights[i][...].reshape(rows, CHANS),
            TN_DIMS,
            preferred_element_type=F32,
        )
        total = part if total is None else total + part
    return total


def inner_kernel(act_ref, own_ref, other_ref, out_ref, here, before, windows):
    core, mine = lax.axis_index("core"), lax.axis_index("y") & 1
    for y in range(LINE):
        where = (y // 2, slice(None), slice((y % 2) * SENT, (y % 2 + 1) * SENT))
        here[where] = act_ref[core, SLOT[y]]

        @pl.when(core == 1)
        def _():
            before[where] = act_ref[0, SLOT[y]]

        @pl.when(core == 0)
        def _():
            before[where] = act_ref[1, SLOT[y - 1]] if y else jnp.zeros_like(act_ref[1, 0])

    now = here[...].reshape(PAIRS * 2 * PART, 2 * SENT)
    prior = before[...].reshape(PAIRS * 2 * PART, 2 * SENT)
    picks = window_picks()
    earliest = jnp.dot(prior, picks, preferred_element_type=F32)
    latest = jnp.dot(now, picks, preferred_element_type=F32)
    lanes = 2 * CELLS
    step = lanes // 4
    frame = (lax.broadcasted_iota(jnp.int32, (PAIRS * 2 * PART, lanes), 1) >> 5) & 1
    for tap in range(9):
        first = earliest[:, tap * lanes : (tap + 1) * lanes]
        last = latest[:, tap * lanes : (tap + 1) * lanes]
        middle = jnp.where(
            frame == 0, pltpu.roll(first, lanes - step, 1), pltpu.roll(last, step, 1)
        )
        for dt, taken in enumerate((first, middle, last)):
            taken = taken.astype(BF16)
            for pair in range(PAIRS):
                for part in range(2):
                    row = (2 * pair + part) * PART
                    windows[
                        part,
                        (9 * dt + tap) * PART : (9 * dt + tap + 1) * PART,
                        pair * lanes : (pair + 1) * lanes,
                    ] = taken[row : row + PART]
    sums = weight_dots(windows, (own_ref, other_ref), mine).astype(BF16)
    for y in range(LINE):
        out_ref[SLOT[y]] = sums[y * CELLS : (y + 1) * CELLS]


def block_kernel(part_ref, lat_ref, bias_ref, later_ref, out_ref, far_ref, near_ref):
    del later_ref
    bias = bias_ref[...].reshape(1, CHANS)
    odd = lax.axis_index("x") & 1
    for half in range(2):
        total = part_ref[SLOT[half]].astype(F32)
        for y in range(half + 2, LINE, 2):
            total = total + part_ref[SLOT[y]].astype(F32)
        total = total + bias
        for f in range(FRAMES):
            for inside in range(HALF):
                row = half * HALF + inside
                start = (f * HALF + inside) * COLS
                value = lat_ref[f, row].astype(F32) + total[start : start + COLS]
                out_ref[f, row] = value.astype(BF16)

    @pl.when(odd == 1)
    def _():
        far_ref[...] = out_ref[:, ROWS - 1]
        near_ref[...] = out_ref[:, 0]

    @pl.when(odd == 0)
    def _():
        far_ref[...] = out_ref[:, 0]
        near_ref[...] = out_ref[:, ROWS - 1]


def upper_inner_kernel(block_ref, weight_ref, out_ref):
    rows = jnp.dot(
        row_picks(), block_ref[...].reshape(SENT, CHANS), preferred_element_type=F32
    ).astype(BF16)
    cells = COLS * FRAMES * 2 * ROWS
    total = None
    for dy in range(3):
        part = lax.dot_general(
            rows[dy * cells : (dy + 1) * cells],
            weight_ref[3 * dy : 3 * dy + 3].reshape(6 * OUTS, CHANS),
            NT_DIMS,
            preferred_element_type=F32,
        )
        total = part if total is None else total + part
    out_ref[...] = total.reshape(out_ref.shape)


def upper_kernel(far_ref, near_ref, inner_ref, weight_ref, bias_ref, out_ref):
    wide = 2 * OUTS
    lines = FRAMES * 2 * ROWS

    far = far_ref[...].reshape(FRAMES * COLS, CHANS).astype(F32)
    near = near_ref[...].reshape(FRAMES * COLS, CHANS).astype(F32)
    odd = lax.axis_index("x") & 1

    def taps(row, dy):
        return lax.dot_general(
            row.astype(BF16),
            weight_ref[3 * dy : 3 * dy + 3].reshape(3 * wide, CHANS),
            NT_DIMS,
            preferred_element_type=F32,
        )

    above = taps(jnp.where(odd == 1, near, far), 0)
    below = taps(jnp.where(odd == 1, far, near), 2)
    line = lax.broadcasted_iota(jnp.int32, (lines, 3 * wide), 0)
    totals = []
    for c in range(COLS):
        total = inner_ref[c]
        for f in range(FRAMES):
            row = f * COLS + c
            top, bottom = f * 2 * ROWS, (f + 1) * 2 * ROWS - 1
            total = total + jnp.where(line == top, above[row : row + 1], 0.0)
            total = total + jnp.where(line == bottom, below[row : row + 1], 0.0)
        totals.append(total)
    bias = bias_ref[...].reshape(1, OUTS)
    bias = jnp.concatenate([bias, bias], axis=1)
    left = lax.broadcasted_iota(jnp.int32, (lines, wide), 1) < OUTS
    zero = jnp.zeros((lines, wide), F32)
    for c in range(COLS):
        first_before = totals[c - 1][:, :wide] if c else zero
        last_after = totals[c + 1][:, 2 * wide :] if c < COLS - 1 else zero
        value = (
            jnp.where(left, first_before, totals[c][:, :wide])
            + totals[c][:, wide : 2 * wide]
            + jnp.where(left, totals[c][:, 2 * wide :], last_after)
            + bias
        )
        out_ref[:, c * wide : (c + 1) * wide] = value.astype(BF16)


def swapped(row, first):
    axes = ("z", "x")
    pairs = []
    for i in range(first, lax.axis_size(axes) - 1, 2):
        pairs += [(i, i + 1), (i + 1, i)]
    return lax.ppermute(row, axes, pairs)


def along_line(blocks):
    return lax.all_to_all(blocks, "y", 0, 0, tiled=True, axis_index_groups=[list(ORDER)])


def call(kernel, outs, inputs, scratch=(), limit=16):
    spaces = [pltpu.HBM if far else pltpu.VMEM for _, far in inputs]
    return pl.pallas_call(
        kernel,
        out_shape=[jax.ShapeDtypeStruct(shape, kind) for shape, kind in outs],
        in_specs=[pl.BlockSpec(memory_space=space) for space in spaces],
        out_specs=[pl.BlockSpec(memory_space=pltpu.VMEM) for _ in outs],
        scratch_shapes=list(scratch),
        compiler_params=pltpu.CompilerParams(vmem_limit_bytes=limit * 1024 * 1024),
    )(*[array for array, _ in inputs])


def local(latent, gain_first, conv_first, bias_first, conv_upper, bias_upper):
    odd = (lax.axis_index("x") & 1) == 1
    first, last = latent[:, 0], latent[:, ROWS - 1]
    far, near = jnp.where(odd, last, first), jnp.where(odd, first, last)
    far, near, conv_first = lax.optimization_barrier((far, near, conv_first))
    far, near = swapped(far, 1), swapped(near, 0)
    other = lax.ppermute(conv_first, "y", [(i, i ^ 1) for i in range(LINE)])
    (own_acts,) = call(
        own_kernel, [((SENT, CHANS), F32)], [(latent, False), (gain_first, False)]
    )
    (acts,) = call(
        act_kernel,
        [((LINE, 2 * PART, SENT), BF16)],
        [(array, False) for array in (far, near, own_acts, gain_first)],
    )
    acts, conv_first, conv_upper = lax.optimization_barrier((acts, conv_first, conv_upper))
    own = lax.all_gather(conv_first, "core", axis=1, tiled=True)
    other = lax.all_gather(other, "core", axis=1, tiled=True)
    upper = jnp.swapaxes(conv_upper, 1, 2)
    upper = jnp.concatenate([upper, upper], axis=1)
    acts = along_line(acts)
    acts, own, other = lax.optimization_barrier((acts, own, other))
    acts = lax.all_gather(acts, "core", axis=0, tiled=False)
    (parts,) = call(
        inner_kernel,
        [((LINE, CELLS, CHANS), BF16)],
        [(acts, False), (own, False), (other, False)],
        [
            pltpu.VMEM((PAIRS, 2 * PART, 2 * SENT), BF16),
            pltpu.VMEM((PAIRS, 2 * PART, 2 * SENT), BF16),
            pltpu.VMEM((2, 27 * PART, LINE * CELLS), BF16),
        ],
        limit=24,
    )
    parts = along_line(parts)
    row = ((FRAMES, COLS, CHANS), BF16)
    block, far, near = call(
        block_kernel,
        [((FRAMES, ROWS, COLS, CHANS), BF16), row, row],
        [(parts, False), (latent, False), (bias_first, False), (upper, True)],
    )
    far, near = swapped(far, 1), swapped(near, 0)
    (inner,) = call(
        upper_inner_kernel,
        [((COLS, FRAMES * 2 * ROWS, 6 * OUTS), F32)],
        [(block, False), (upper, False)],
    )
    (out,) = call(
        upper_kernel,
        [((FRAMES * 2 * ROWS, 2 * COLS * OUTS), BF16)],
        [(array, False) for array in (far, near, inner, upper, bias_upper)],
    )
    return out.reshape(FRAMES, 2 * ROWS, 2 * COLS * OUTS)


def solution(mesh):
    fine = Mesh(mesh.devices.reshape(8, 2, 8, 4), ("y", "core", "z", "x"))
    tm, rows = ("y", "core"), ("z", "x")
    in_specs = (P(tm, rows, None, None), P(), P(None, tm, None), P(), P(), P())
    return jax.shard_map(
        local, mesh=fine, in_specs=in_specs, out_specs=P(tm, rows, None), check_vma=False
    )
```

```python
import jax
import jax.numpy as jnp
from jax import lax
from jax.experimental import pallas as pl
from jax.experimental.pallas import tpu as pltpu
from jax.sharding import Mesh
from jax.sharding import PartitionSpec as P

F32 = jnp.float32
BF16 = jnp.bfloat16
FRAMES, ROWS, COLS, CHANS, OUTS = 2, 4, 16, 384, 192
LINE = 8
PART = CHANS // LINE
PAIRS = LINE // 2
HALF = ROWS // 2
CELLS = FRAMES * HALF * COLS
SENT = FRAMES * ROWS * COLS
ORDER = (4, 6, 0, 2, 5, 7, 1, 3)
SLOT = tuple(ORDER.index(y) for y in range(LINE))
NT_DIMS = (((1,), (1,)), ((), ()))
TN_DIMS = (((0,), (0,)), ((), ()))


def one_hot(wanted, there):
    return jnp.where(wanted == there, 1.0, 0.0).astype(BF16)


def window_picks():
    lane = lax.broadcasted_iota(jnp.int32, (1, 18 * CELLS), 1)
    tap, frame, row, col = lane >> 7, (lane >> 5) & 3, (lane >> 4) & 1, lane & 15
    dy = (tap * 11) >> 5
    col = col + tap - 3 * dy - 1
    wanted = (frame << 6) + ((row + dy) << 4) + col
    wanted = jnp.where((col >= 0) & (col < COLS), wanted, -1)
    return one_hot(wanted, lax.broadcasted_iota(jnp.int32, (2 * SENT, 18 * CELLS), 0))


def row_picks():
    shape = (6 * ROWS * COLS * FRAMES, SENT)
    place = lax.broadcasted_iota(jnp.int32, (shape[0], 1), 0)
    dy, col, frame, i = place >> 8, (place >> 4) & 15, (place >> 3) & 1, place & 7
    row = ((i + dy + 1) >> 1) - 1
    wanted = (frame << 6) + (row << 4) + col
    wanted = jnp.where((row >= 0) & (row < ROWS), wanted, -1)
    return one_hot(wanted, lax.broadcasted_iota(jnp.int32, shape, 1))


def scaled_silu(block, gain):
    values = block.astype(F32)
    mean_square = jnp.mean(values * values, axis=-1, keepdims=True)
    scaled = values * lax.rsqrt(mean_square + 1e-06) * gain
    return scaled / (1.0 + jnp.exp(-scaled))


def own_kernel(lat_ref, gain_ref, out_ref):
    out_ref[...] = scaled_silu(
        lat_ref[...].reshape(SENT, CHANS), gain_ref[...].reshape(1, CHANS)
    )


def act_kernel(far_ref, near_ref, own_ref, gain_ref, out_ref):
    odd = lax.axis_index("x") & 1
    count = FRAMES * COLS
    far = far_ref[...].reshape(count, CHANS).astype(F32)
    near = near_ref[...].reshape(count, CHANS).astype(F32)
    edges = jnp.concatenate(
        [jnp.where(odd == 1, near, far), jnp.where(odd == 1, far, near)], axis=0
    )
    edges = scaled_silu(edges, gain_ref[...].reshape(1, CHANS))
    own = own_ref[...]
    size = (HALF + 1) * COLS
    for half in range(2):
        cells = []
        for f in range(FRAMES):
            start = (f * ROWS + half * (HALF - 1)) * COLS
            beside = (half * FRAMES + f) * COLS
            parts = [edges[beside : beside + COLS], own[start : start + size]]
            cells += parts if half == 0 else parts[::-1]
        flipped = jnp.concatenate(cells, axis=0).T.astype(BF16)
        for pair in range(PAIRS):
            start = pair * 2 * PART
            out_ref[SLOT[2 * pair + half]] = flipped[start : start + 2 * PART]


def weight_dots(blocks, weights, mine):
    total = None
    for i in range(2):
        rows = blocks.shape[1]
        part = lax.dot_general(
            blocks[mine if i == 0 else 1 - mine],
            weights[i][...].reshape(rows, CHANS),
            TN_DIMS,
            preferred_element_type=F32,
        )
        total = part if total is None else total + part
    return total


def inner_kernel(act_ref, own_ref, other_ref, out_ref, here, before, windows):
    core, mine = lax.axis_index("core"), lax.axis_index("y") & 1
    for y in range(LINE):
        where = (y // 2, slice(None), slice((y % 2) * SENT, (y % 2 + 1) * SENT))
        here[where] = act_ref[core, SLOT[y]]

        @pl.when(core == 1)
        def _():
            before[where] = act_ref[0, SLOT[y]]

        @pl.when(core == 0)
        def _():
            before[where] = act_ref[1, SLOT[y - 1]] if y else jnp.zeros_like(act_ref[1, 0])

    now = here[...].reshape(PAIRS * 2 * PART, 2 * SENT)
    prior = before[...].reshape(PAIRS * 2 * PART, 2 * SENT)
    picks = window_picks()
    earliest = jnp.dot(prior, picks, preferred_element_type=F32)
    latest = jnp.dot(now, picks, preferred_element_type=F32)
    lanes = 2 * CELLS
    step = lanes // 4
    frame = (lax.broadcasted_iota(jnp.int32, (PAIRS * 2 * PART, lanes), 1) >> 5) & 1
    for tap in range(9):
        first = earliest[:, tap * lanes : (tap + 1) * lanes]
        last = latest[:, tap * lanes : (tap + 1) * lanes]
        middle = jnp.where(
            frame == 0, pltpu.roll(first, lanes - step, 1), pltpu.roll(last, step, 1)
        )
        for dt, taken in enumerate((first, middle, last)):
            taken = taken.astype(BF16)
            for pair in range(PAIRS):
                for part in range(2):
                    row = (2 * pair + part) * PART
                    windows[
                        part,
                        (9 * dt + tap) * PART : (9 * dt + tap + 1) * PART,
                        pair * lanes : (pair + 1) * lanes,
                    ] = taken[row : row + PART]
    sums = weight_dots(windows, (own_ref, other_ref), mine).astype(BF16)
    for y in range(LINE):
        out_ref[SLOT[y]] = sums[y * CELLS : (y + 1) * CELLS]


def block_kernel(part_ref, lat_ref, bias_ref, later_ref, out_ref, far_ref, near_ref):
    del later_ref
    bias = bias_ref[...].reshape(1, CHANS)
    odd = lax.axis_index("x") & 1
    for half in range(2):
        total = part_ref[SLOT[half]].astype(F32)
        for y in range(half + 2, LINE, 2):
            total = total + part_ref[SLOT[y]].astype(F32)
        total = total + bias
        for f in range(FRAMES):
            for inside in range(HALF):
                row = half * HALF + inside
                start = (f * HALF + inside) * COLS
                value = lat_ref[f, row].astype(F32) + total[start : start + COLS]
                out_ref[f, row] = value.astype(BF16)

    @pl.when(odd == 1)
    def _():
        far_ref[...] = out_ref[:, ROWS - 1]
        near_ref[...] = out_ref[:, 0]

    @pl.when(odd == 0)
    def _():
        far_ref[...] = out_ref[:, 0]
        near_ref[...] = out_ref[:, ROWS - 1]


def upper_inner_kernel(block_ref, weight_ref, bias_ref, out_ref):
    rows = jnp.dot(
        row_picks(), block_ref[...].reshape(SENT, CHANS), preferred_element_type=F32
    ).astype(BF16)
    cells = COLS * FRAMES * 2 * ROWS
    total = None
    for dy in range(3):
        part = lax.dot_general(
            rows[dy * cells : (dy + 1) * cells],
            weight_ref[3 * dy : 3 * dy + 3].reshape(6 * OUTS, CHANS),
            NT_DIMS,
            preferred_element_type=F32,
        )
        total = part if total is None else total + part
    bias = bias_ref[...].reshape(1, OUTS)
    zero = jnp.zeros((1, 2 * OUTS), F32)
    total = total + jnp.concatenate([zero, bias, bias, zero], axis=1)
    out_ref[...] = total.reshape(out_ref.shape)


def upper_kernel(far_ref, near_ref, inner_ref, weight_ref, out_ref):
    wide = 2 * OUTS
    lines = FRAMES * 2 * ROWS

    far = far_ref[...].reshape(FRAMES * COLS, CHANS).astype(F32)
    near = near_ref[...].reshape(FRAMES * COLS, CHANS).astype(F32)
    odd = lax.axis_index("x") & 1

    def taps(row, dy):
        return lax.dot_general(
            row.astype(BF16),
            weight_ref[3 * dy : 3 * dy + 3].reshape(3 * wide, CHANS),
            NT_DIMS,
            preferred_element_type=F32,
        )

    above = taps(jnp.where(odd == 1, near, far), 0)
    below = taps(jnp.where(odd == 1, far, near), 2)
    line = lax.broadcasted_iota(jnp.int32, (lines, 3 * wide), 0)
    totals = []
    for c in range(COLS):
        beside = 0.0
        for f in range(FRAMES):
            row = f * COLS + c
            top, bottom = f * 2 * ROWS, (f + 1) * 2 * ROWS - 1
            beside = jnp.where(line == top, above[row : row + 1], beside)
            beside = jnp.where(line == bottom, below[row : row + 1], beside)
        totals.append(inner_ref[c] + beside)
    left = lax.broadcasted_iota(jnp.int32, (lines, wide), 1) < OUTS
    zero = jnp.zeros((lines, wide), F32)
    for c in range(COLS):
        first_before = totals[c - 1][:, :wide] if c else zero
        last_after = totals[c + 1][:, 2 * wide :] if c < COLS - 1 else zero
        value = (
            jnp.where(left, first_before, totals[c][:, :wide])
            + totals[c][:, wide : 2 * wide]
            + jnp.where(left, totals[c][:, 2 * wide :], last_after)
        )
        out_ref[:, c * wide : (c + 1) * wide] = value.astype(BF16)


def swapped(row, first):
    axes = ("z", "x")
    pairs = []
    for i in range(first, lax.axis_size(axes) - 1, 2):
        pairs += [(i, i + 1), (i + 1, i)]
    return lax.ppermute(row, axes, pairs)


def along_line(blocks):
    return lax.all_to_all(blocks, "y", 0, 0, tiled=True, axis_index_groups=[list(ORDER)])


def call(kernel, outs, inputs, scratch=(), limit=16):
    spaces = [pltpu.HBM if far else pltpu.VMEM for _, far in inputs]
    return pl.pallas_call(
        kernel,
        out_shape=[jax.ShapeDtypeStruct(shape, kind) for shape, kind in outs],
        in_specs=[pl.BlockSpec(memory_space=space) for space in spaces],
        out_specs=[pl.BlockSpec(memory_space=pltpu.VMEM) for _ in outs],
        scratch_shapes=list(scratch),
        compiler_params=pltpu.CompilerParams(vmem_limit_bytes=limit * 1024 * 1024),
    )(*[array for array, _ in inputs])


def local(latent, gain_first, conv_first, bias_first, conv_upper, bias_upper):
    odd = (lax.axis_index("x") & 1) == 1
    first, last = latent[:, 0], latent[:, ROWS - 1]
    far, near = jnp.where(odd, last, first), jnp.where(odd, first, last)
    far, near, conv_first = lax.optimization_barrier((far, near, conv_first))
    far, near = swapped(far, 1), swapped(near, 0)
    other = lax.ppermute(conv_first, "y", [(i, i ^ 1) for i in range(LINE)])
    (own_acts,) = call(
        own_kernel, [((SENT, CHANS), F32)], [(latent, False), (gain_first, False)]
    )
    (acts,) = call(
        act_kernel,
        [((LINE, 2 * PART, SENT), BF16)],
        [(array, False) for array in (far, near, own_acts, gain_first)],
    )
    acts, conv_first, conv_upper = lax.optimization_barrier((acts, conv_first, conv_upper))
    own = lax.all_gather(conv_first, "core", axis=1, tiled=True)
    other = lax.all_gather(other, "core", axis=1, tiled=True)
    upper = jnp.swapaxes(conv_upper, 1, 2)
    upper = jnp.concatenate([upper, upper], axis=1)
    acts = along_line(acts)
    acts, own, other = lax.optimization_barrier((acts, own, other))
    acts = lax.all_gather(acts, "core", axis=0, tiled=False)
    (parts,) = call(
        inner_kernel,
        [((LINE, CELLS, CHANS), BF16)],
        [(acts, False), (own, False), (other, False)],
        [
            pltpu.VMEM((PAIRS, 2 * PART, 2 * SENT), BF16),
            pltpu.VMEM((PAIRS, 2 * PART, 2 * SENT), BF16),
            pltpu.VMEM((2, 27 * PART, LINE * CELLS), BF16),
        ],
        limit=24,
    )
    parts = along_line(parts)
    row = ((FRAMES, COLS, CHANS), BF16)
    block, far, near = call(
        block_kernel,
        [((FRAMES, ROWS, COLS, CHANS), BF16), row, row],
        [(parts, False), (latent, False), (bias_first, False), (upper, True)],
    )
    far, near = swapped(far, 1), swapped(near, 0)
    (inner,) = call(
        upper_inner_kernel,
        [((COLS, FRAMES * 2 * ROWS, 6 * OUTS), F32)],
        [(block, False), (upper, False), (bias_upper, False)],
    )
    (out,) = call(
        upper_kernel,
        [((FRAMES * 2 * ROWS, 2 * COLS * OUTS), BF16)],
        [(array, False) for array in (far, near, inner, upper)],
    )
    return out.reshape(FRAMES, 2 * ROWS, 2 * COLS * OUTS)


def solution(mesh):
    fine = Mesh(mesh.devices.reshape(8, 2, 8, 4), ("y", "core", "z", "x"))
    tm, rows = ("y", "core"), ("z", "x")
    in_specs = (P(tm, rows, None, None), P(), P(None, tm, None), P(), P(), P())
    return jax.shard_map(
        local, mesh=fine, in_specs=in_specs, out_specs=P(tm, rows, None), check_vma=False
    )
```
